32 devices in a mesh: blk: 8 (over z, y), grp: 4 (over x, core).
Axes of the slice: x: 2, y: 2, z: 4, core: 2. Of those that a mesh axis runs over, the one named last changes fastest.
Arguments:
- features: bfloat16 [24576, 2048], P(('blk', 'grp'))
- factors: bfloat16 [24576, 512], P(('blk', 'grp'))
- pivots: int32 [2, 256], replicated, may hold values from 0 to 767, as said below
- owners: int32 [2], replicated, may hold values from 0 to 31, as said below
Outputs:
- embedding: float32 [24576], P(('blk', 'grp'))
- columns: bfloat16 [24576, 512], P(('blk', 'grp'))
- leftover: float32 [24576], P(('blk', 'grp'))
The draws below stay inside these ranges and needn't reach their ends.
Inputs may be any that keep to these rules, and one draw needn't show every extreme that they name: `pivots`: each row holds 256 distinct row numbers from 0 to 767. The 2 owners are distinct devices; one of them is the last device.
All inputs are finite; a program needn't handle non-finite values.
Results may differ from the reference program's by a relative error of at most 0.001.
Values may be sent and summed in bfloat16 or wider, within the bound.
A program may use at most 64 MiB of HBM per device.

```python
import math
import jax
import jax.numpy as jnp
from jax import lax

F = 2048
PIV = 256
R0 = 512
ROUNDS = 2
S = 768
NSCEN = 24576
N_BLK = 8
N_GRP = 4


def draw_features(key, part):
    kcent, kpick, kwhich, kcoef, knoise, katom = jax.random.split(jax.random.fold_in(key, 11), 6)
    row_count = S * N_BLK * N_GRP
    per_block = max(S // 32, 1)
    cluster_count = N_BLK * per_block
    row_ids = jnp.arange(row_count, dtype=jnp.int32)
    block_numbers = row_ids // (N_GRP * S)
    grp_ids = row_ids // S % N_GRP
    offsets = jax.random.randint(kwhich, (row_count,), 0, 3 * per_block, dtype=jnp.int32)
    cluster = grp_ids * cluster_count + (block_numbers * per_block + offsets) % cluster_count
    selected_atoms = jax.random.randint(kpick, (N_GRP * cluster_count, 8), 0, F, dtype=jnp.int32)
    centres = jax.random.normal(kcent, (N_GRP * cluster_count, F), jnp.float32)
    atoms = jax.random.normal(katom, (F, F), jnp.float32)
    weights = jax.random.normal(kcoef, (row_count, 8), jnp.float32)
    noise = jax.random.normal(knoise, (row_count, F), jnp.float32)
    feat = 4.05 * centres[cluster] + 1.789 * noise
    chosen = selected_atoms[cluster]
    for column in range(8):
        feat = feat + 0.5477 * weights[:, column:column + 1] * atoms[chosen[:, column]]
    return feat.astype(jnp.bfloat16)


def draw_factors(key, part):
    scale_random_key, value_random_key = jax.random.split(jax.random.fold_in(key, 23), 2)
    grand_total = S * N_BLK * N_GRP
    noise_level = jnp.exp(jax.random.uniform(scale_random_key, (grand_total, 1), jnp.float32, math.log(0.01), math.log(0.16)))
    vals = jax.random.uniform(value_random_key, (grand_total, R0), jnp.float32, -1.7320508, 1.7320508)
    return (vals * jnp.sqrt(noise_level / R0)).astype(jnp.bfloat16)


def draw_pivots(key, part):
    rows = []
    for rnd in range(ROUNDS):
        order = jax.random.permutation(jax.random.fold_in(key, 31 + rnd), S)
        rows.append(order[:PIV])
    return jnp.stack(rows).astype(jnp.int32)


def draw_owners(key, part):
    device_count = N_BLK * N_GRP
    others = jax.random.permutation(jax.random.fold_in(key, 47), device_count - 1)[:ROUNDS - 1].astype(jnp.int32)
    picked = jnp.concatenate([others, jnp.full((1,), device_count - 1, dtype=jnp.int32)])
    placing = jax.random.permutation(jax.random.fold_in(key, 53), ROUNDS)
    return picked[placing].astype(jnp.int32)


def setup_inputs(seed: int = 0) -> dict:
    splits = jax.random.split(jax.random.key(seed), 5)
    return {
        "features": draw_features(jax.random.fold_in(splits[4], 71), 0),
        "factors": draw_factors(jax.random.fold_in(splits[4], 71), 0),
        "pivots": draw_pivots(jax.random.fold_in(splits[4], 71), 0),
        "owners": draw_owners(jax.random.fold_in(splits[4], 71), 0),
    }


def squares(block):
    wide = block.astype(jnp.float32)
    return jnp.sum(wide * wide, axis=1)

def kernel_block(left, right, left_sq, right_sq):
    gram = jnp.dot(left.astype(jnp.float32), right.T.astype(jnp.float32), preferred_element_type=jnp.float32)
    dist = left_sq[:, None] + right_sq[None, :] - 2.0 * gram
    return jnp.exp(-dist / (8.0 * F))

def solve_block(piv_x, piv_sq, piv_l):
    schur = kernel_block(piv_x, piv_x, piv_sq, piv_sq) - jnp.dot(piv_l.astype(jnp.float32), piv_l.T.astype(jnp.float32), preferred_element_type=jnp.float32)
    lower = jnp.linalg.cholesky(schur)
    ident = jnp.eye(schur.shape[0], dtype=jnp.float32)
    return lax.linalg.triangular_solve(lower, ident, left_side=True, lower=True)

def apply_block(tx, tsq, tl, piv_x, piv_sq, piv_l, inverse):
    cross = kernel_block(tx, piv_x, tsq, piv_sq) - jnp.dot(tl.astype(jnp.float32), piv_l.T.astype(jnp.float32), preferred_element_type=jnp.float32)
    return jnp.dot(cross.astype(jnp.float32), inverse.T.astype(jnp.float32), precision=lax.Precision.HIGHEST, preferred_element_type=jnp.float32).astype(jnp.bfloat16)

def reference(features, factors, pivots, owners):
    devices = N_BLK * N_GRP
    blocks = features.reshape(N_BLK, N_GRP, S, F)

    def embed_one(index):
        bidx = index // N_GRP
        gidx = index % N_GRP
        own = blocks[bidx, gidx]
        own_sq = squares(own)
        grand_total = jnp.sum(kernel_block(own, own, own_sq, own_sq), axis=1)
        for step in (1, 2):
            other = blocks[(bidx - step) % N_BLK, gidx]
            grand_total = grand_total + jnp.sum(kernel_block(own, other, own_sq, squares(other)), axis=1)
        return grand_total / (3.0 * S)
    embedding = lax.map(embed_one, jnp.arange(devices, dtype=jnp.int32)).reshape(-1)
    flat = features.reshape(devices, S, F)
    current = factors
    newcols = []
    for rnd in range(ROUNDS):
        rows = (owners[rnd] * S + pivots[rnd]).astype(jnp.int32)
        piv_x = features[rows]
        piv_l = current[rows]
        piv_sq = squares(piv_x)
        inverse = solve_block(piv_x, piv_sq, piv_l)
        width = current.shape[1]

        def extend_one(pair):
            return apply_block(pair[0], squares(pair[0]), pair[1], piv_x, piv_sq, piv_l, inverse)
        fresh = lax.map(extend_one, (flat, current.reshape(devices, S, width))).reshape(NSCEN, PIV)
        newcols.append(fresh)
        current = jnp.concatenate([current, fresh], axis=1)
    columns = jnp.concatenate(newcols, axis=1)
    wide = current.astype(jnp.float32)
    leftover = 1.0 - jnp.sum(wide * wide, axis=1)
    return (embedding, columns, leftover)
```

```python
import functools

import jax
import jax.numpy as jnp
from jax import lax
from jax.experimental import pallas as pl
from jax.experimental.pallas import tpu as pltpu
from jax.sharding import PartitionSpec as P

ROUNDS = 2
F32 = jnp.float32
BF16 = jnp.bfloat16
HIGHEST = lax.Precision.HIGHEST
VMEM_LIMIT = 56 * 1024 * 1024
NT = (((1,), (1,)), ((), ()))
TN = (((0,), (0,)), ((), ()))


def dot_nt(a, b):
    return lax.dot_general(a, b, NT, preferred_element_type=F32)


def dot_nt_high(a, b):
    return lax.dot_general(a, b, NT, precision=HIGHEST, preferred_element_type=F32)


def split3(x):
    high = x.astype(BF16).astype(F32)
    rest = x - high
    mid = rest.astype(BF16).astype(F32)
    return high, mid, rest - mid


def factor(a_ref, m_ref, inv_ref):
    n = a_ref.shape[0]
    half = 128
    row = lax.broadcasted_iota(jnp.int32, (n, n), 0)
    col = lax.broadcasted_iota(jnp.int32, (n, n), 1)
    m_ref[...] = (row == col).astype(F32)
    inv_ref[...] = jnp.zeros((n, n), F32)
    sub = lax.broadcasted_iota(jnp.int32, (8, 128), 0)

    for part in range(n // half):
        left = part * half
        right = left + half
        wide = n - left
        lane = lax.broadcasted_iota(jnp.int32, (8, half), 1)

        def panel(k, carry):
            base = pl.multiple_of(left + k * 8, 8)
            rows = pl.ds(base, 8)
            panel_a = a_ref[rows, left:]
            panel_m = m_ref[rows, :right]
            diag = panel_a[:, :half]
            tiles = [panel_a[:, t * 128:(t + 1) * 128] for t in range(wide // 128)]
            tiles += [panel_m[:, t * 128:(t + 1) * 128] for t in range(right // 128)]
            cols = []
            for j in range(8):
                picked = jnp.where(lane == k * 8 + j, diag, 0.0)
                cols.append(jnp.broadcast_to(jnp.sum(picked, axis=1, keepdims=True), (8, 128)))
            scale = jnp.ones((8, 128), F32)
            for j in range(8):
                pivot = jnp.broadcast_to(cols[j][j:j + 1, :], (8, 128))
                scale = jnp.where(sub == j, pivot, scale)
                if j < 7:
                    mult = jnp.where(sub > j, cols[j] / pivot, 0.0)
                    for c in range(j + 1, 8):
                        cols[c] = cols[c] - mult * jnp.broadcast_to(cols[c][j:j + 1, :], (8, 128))
                    tiles = [t - mult * jnp.broadcast_to(t[j:j + 1, :], (8, 128)) for t in tiles]
            scale = lax.rsqrt(scale)
            tiles = [t * scale for t in tiles]
            q = jnp.concatenate(tiles, axis=1)
            inv_ref[rows, :right] = q[:, wide:]
            h, m, l = split3(q)
            rhs = jnp.concatenate([h, m, h, l, h, m], axis=0).astype(BF16)
            lhs = jnp.concatenate([h, h, m, h, l, m], axis=0)[:, :wide].astype(BF16)
            upd = lax.dot_general(lhs, rhs, TN, preferred_element_type=F32)
            a_ref[left:, left:] = a_ref[left:, left:] - upd[:, :wide]
            m_ref[left:, :right] = m_ref[left:, :right] - upd[:, wide:]
            return carry

        lax.fori_loop(0, half // 8, panel, 0)


def diagonals(gram):
    n = gram.shape[0]
    row = lax.broadcasted_iota(jnp.int32, (n, n), 0)
    col = lax.broadcasted_iota(jnp.int32, (n, n), 1)
    only = jnp.where(row == col, gram, 0.0)
    return jnp.sum(only, axis=1, keepdims=True), jnp.sum(only, axis=0, keepdims=True)


def closeness(gram, left_sq, right_sq, width):
    return jnp.exp((2.0 * gram - left_sq - right_sq) / (8.0 * width))


def solve_kernel(x_ref, l_ref, inv_ref, ext_ref, sq_ref, a_ref, m_ref):
    width = x_ref.shape[2]
    gram0 = dot_nt(x_ref[0], x_ref[0])
    c0, r0 = diagonals(gram0)
    a_ref[...] = closeness(gram0, c0, r0, width) - dot_nt(l_ref[0], l_ref[0])
    factor(a_ref, m_ref, inv_ref.at[0])
    gram1 = dot_nt(x_ref[1], x_ref[1])
    c1, r1 = diagonals(gram1)
    cross = closeness(dot_nt(x_ref[1], x_ref[0]), c1, r0, width) - dot_nt(l_ref[1], l_ref[0])
    ext = dot_nt_high(cross, inv_ref[0]).astype(BF16)
    ext_ref[...] = ext
    a_ref[...] = closeness(gram1, c1, r1, width) - dot_nt(l_ref[1], l_ref[1]) - dot_nt(ext, ext)
    factor(a_ref, m_ref, inv_ref.at[1])
    sq_ref[...] = jnp.concatenate([r0, r1, jnp.zeros((6, r0.shape[1]), F32)], axis=0)


def solve_pivots(x, l):
    piv = x.shape[1]
    vmem = pl.BlockSpec(memory_space=pltpu.VMEM)
    return pl.pallas_call(
        solve_kernel,
        out_shape=(
            jax.ShapeDtypeStruct((ROUNDS, piv, piv), F32),
            jax.ShapeDtypeStruct((piv, piv), BF16),
            jax.ShapeDtypeStruct((8, piv), F32),
        ),
        in_specs=[vmem, vmem],
        out_specs=(vmem, vmem, vmem),
        scratch_shapes=[pltpu.VMEM((piv, piv), F32), pltpu.VMEM((piv, piv), F32)],
        compiler_params=pltpu.CompilerParams(vmem_limit_bytes=24 * 1024 * 1024),
        cost_estimate=pl.CostEstimate(flops=64 * 10**9, bytes_accessed=2 * 10**6, transcendentals=0),
        name="solve_pivots",
    )(x, l)


def apply_kernel(t_ref, tl_ref, x_ref, l_ref, inv_ref, ext_ref, sq_ref, col_ref, left_ref):
    width = t_ref.shape[1]
    piv = x_ref.shape[1]
    x = t_ref[...]
    wide = x.astype(F32)
    sq = jnp.sum(wide * wide, axis=1, keepdims=True)
    tl = tl_ref[...]
    cross = closeness(dot_nt(x, x_ref[0]), sq, sq_ref[0:1, :], width) - dot_nt(tl, l_ref[0])
    new0 = dot_nt_high(cross, inv_ref[0]).astype(BF16)
    cross = closeness(dot_nt(x, x_ref[1]), sq, sq_ref[1:2, :], width) - dot_nt(tl, l_ref[1]) - dot_nt(
        new0, ext_ref[...]
    )
    new1 = dot_nt_high(cross, inv_ref[1]).astype(BF16)
    col_ref[:, :piv] = new0
    col_ref[:, piv:] = new1
    total = jnp.zeros((x.shape[0], 128), F32)
    for part in (tl, new0, new1):
        part = part.astype(F32)
        part = part * part
        for t in range(part.shape[1] // 128):
            total = total + part[:, t * 128:(t + 1) * 128]
    turned = jnp.transpose(total)
    left_ref[...] = 1.0 - jnp.sum(turned, axis=0, keepdims=True)


def apply_all(features, factors, x, l, inv, ext, sq):
    rows, width = features.shape
    rank = factors.shape[1]
    piv = x.shape[1]
    tile = 256
    vmem = pl.BlockSpec(memory_space=pltpu.VMEM)
    return pl.pallas_call(
        apply_kernel,
        grid=(rows // tile,),
        out_shape=(
            jax.ShapeDtypeStruct((rows, ROUNDS * piv), BF16),
            jax.ShapeDtypeStruct((1, rows), F32),
        ),
        in_specs=[
            pl.BlockSpec((tile, width), lambda i: (i, 0)),
            pl.BlockSpec((tile, rank), lambda i: (i, 0)),
            vmem, vmem, vmem, vmem, vmem,
        ],
        out_specs=(
            pl.BlockSpec((tile, ROUNDS * piv), lambda i: (i, 0)),
            pl.BlockSpec((1, tile), lambda i: (0, i)),
        ),
        compiler_params=pltpu.CompilerParams(vmem_limit_bytes=32 * 1024 * 1024),
        cost_estimate=pl.CostEstimate(flops=3 * 10**9, bytes_accessed=8 * 10**6, transcendentals=0),
        name="apply_pivots",
    )(features, factors, x, l, inv, ext, sq)


def squares(block):
    wide = block.astype(F32)
    return jnp.sum(wide * wide, axis=1)


def kernel_sum(left, right, left_sq):
    gram = jnp.dot(left, right.T, preferred_element_type=F32)
    dist = left_sq[:, None] + squares(right)[None, :] - 2.0 * gram
    return jnp.sum(jnp.exp(-dist / (8.0 * left.shape[1])), axis=1)


def on_device(features, factors, pivots, owners):
    rows = features.shape[0]
    count = lax.axis_size("blk")
    me = lax.axis_index("blk") * lax.axis_size("grp") + lax.axis_index("grp")
    xs, ls = [], []
    for rnd in range(ROUNDS):
        mine = owners[rnd] == me
        xs.append(jnp.where(mine, jnp.take(features, pivots[rnd], axis=0), 0))
        ls.append(jnp.where(mine, jnp.take(factors, pivots[rnd], axis=0), 0))
    x, l = lax.psum((jnp.stack(xs), jnp.stack(ls)), ("blk", "grp"))

    odd = lax.axis_index("blk") % 2 == 1
    two_on = [(b, (b + 2) % count) for b in range(count)]
    swap = [(b, b ^ 1) for b in range(count)]
    chunks = 4
    size = rows // chunks
    own_sq = squares(features)
    total = kernel_sum(features, features, own_sq)
    for c in range(chunks):
        piece = lax.slice_in_dim(features, c * size, (c + 1) * size)
        second = lax.ppermute(piece, "blk", two_on)
        first = lax.ppermute(jnp.where(odd, second, piece), "blk", swap)
        total = total + kernel_sum(features, second, own_sq) + kernel_sum(features, first, own_sq)
    embedding = total / (3.0 * rows)

    inv, ext, sq = solve_pivots(x, l)
    columns, leftover = apply_all(features, factors, x, l, inv, ext, sq)
    return embedding, columns, leftover.reshape(rows)


def solution(mesh):
    placed = (P(("blk", "grp"), None), P(("blk", "grp"), None), P(), P())
    return jax.shard_map(
        on_device,
        mesh=mesh,
        in_specs=placed,
        out_specs=(P(("blk", "grp")), P(("blk", "grp"), None), P(("blk", "grp"))),
        check_vma=False,
    )
```

```python
import functools

import jax
import jax.numpy as jnp
from jax import lax
from jax.experimental import pallas as pl
from jax.experimental.pallas import tpu as pltpu
from jax.sharding import PartitionSpec as P

ROUNDS = 2
F32 = jnp.float32
BF16 = jnp.bfloat16
HIGHEST = lax.Precision.HIGHEST
VMEM_LIMIT = 56 * 1024 * 1024
NT = (((1,), (1,)), ((), ()))
TN = (((0,), (0,)), ((), ()))


def dot_nt(a, b):
    return lax.dot_general(a, b, NT, preferred_element_type=F32)


def dot_nt_high(a, b):
    return lax.dot_general(a, b, NT, precision=HIGHEST, preferred_element_type=F32)


def split3(x):
    high = x.astype(BF16).astype(F32)
    rest = x - high
    mid = rest.astype(BF16).astype(F32)
    return high, mid, rest - mid


def factor(a_ref, m_ref, inv_ref):
    n = a_ref.shape[0]
    half = 128
    row = lax.broadcasted_iota(jnp.int32, (n, n), 0)
    col = lax.broadcasted_iota(jnp.int32, (n, n), 1)
    m_ref[...] = (row == col).astype(F32)
    inv_ref[...] = jnp.zeros((n, n), F32)
    sub = lax.broadcasted_iota(jnp.int32, (8, 128), 0)

    for part in range(n // half):
        left = part * half
        right = left + half
        wide = n - left
        lane = lax.broadcasted_iota(jnp.int32, (8, half), 1)

        def panel(k, carry):
            base = pl.multiple_of(left + k * 8, 8)
            rows = pl.ds(base, 8)
            panel_a = a_ref[rows, left:]
            panel_m = m_ref[rows, :right]
            diag = panel_a[:, :half]
            tiles = [panel_a[:, t * 128:(t + 1) * 128] for t in range(wide // 128)]
            tiles += [panel_m[:, t * 128:(t + 1) * 128] for t in range(right // 128)]
            cols = []
            for j in range(8):
                picked = jnp.where(lane == k * 8 + j, diag, 0.0)
                cols.append(jnp.broadcast_to(jnp.sum(picked, axis=1, keepdims=True), (8, 128)))
            scale = jnp.ones((8, 128), F32)
            for j in range(8):
                pivot = jnp.broadcast_to(cols[j][j:j + 1, :], (8, 128))
                scale = jnp.where(sub == j, pivot, scale)
                if j < 7:
                    mult = jnp.where(sub > j, cols[j] / pivot, 0.0)
                    for c in range(j + 1, 8):
                        cols[c] = cols[c] - mult * jnp.broadcast_to(cols[c][j:j + 1, :], (8, 128))
                    tiles = [t - mult * jnp.broadcast_to(t[j:j + 1, :], (8, 128)) for t in tiles]
            scale = lax.rsqrt(scale)
            tiles = [t * scale for t in tiles]
            q = jnp.concatenate(tiles, axis=1)
            inv_ref[rows, :right] = q[:, wide:]
            h, m, l = split3(q)
            rhs = jnp.concatenate([h, m, h, l, h, m], axis=0).astype(BF16)
            lhs = jnp.concatenate([h, h, m, h, l, m], axis=0)[:, :wide].astype(BF16)
            upd = lax.dot_general(lhs, rhs, TN, preferred_element_type=F32)
            a_ref[left:, left:] = a_ref[left:, left:] - upd[:, :wide]
            m_ref[left:, :right] = m_ref[left:, :right] - upd[:, wide:]
            return carry

        lax.fori_loop(0, half // 8, panel, 0)


def diagonals(gram):
    n = gram.shape[0]
    row = lax.broadcasted_iota(jnp.int32, (n, n), 0)
    col = lax.broadcasted_iota(jnp.int32, (n, n), 1)
    only = jnp.where(row == col, gram, 0.0)
    return jnp.sum(only, axis=1, keepdims=True), jnp.sum(only, axis=0, keepdims=True)


def closeness(gram, left_sq, right_sq, width):
    return jnp.exp((2.0 * gram - left_sq - right_sq) / (8.0 * width))


def solve_kernel(x_ref, l_ref, inv_ref, ext_ref, sq_ref, a_ref, m_ref):
    width = x_ref.shape[2]
    gram0 = dot_nt(x_ref[0], x_ref[0])
    c0, r0 = diagonals(gram0)
    a_ref[...] = closeness(gram0, c0, r0, width) - dot_nt(l_ref[0], l_ref[0])
    factor(a_ref, m_ref, inv_ref.at[0])
    gram1 = dot_nt(x_ref[1], x_ref[1])
    c1, r1 = diagonals(gram1)
    cross = closeness(dot_nt(x_ref[1], x_ref[0]), c1, r0, width) - dot_nt(l_ref[1], l_ref[0])
    ext = dot_nt_high(cross, inv_ref[0]).astype(BF16)
    ext_ref[...] = ext
    a_ref[...] = closeness(gram1, c1, r1, width) - dot_nt(l_ref[1], l_ref[1]) - dot_nt(ext, ext)
    factor(a_ref, m_ref, inv_ref.at[1])
    sq_ref[...] = jnp.concatenate([r0, r1, jnp.zeros((6, r0.shape[1]), F32)], axis=0)


def solve_pivots(x, l):
    piv = x.shape[1]
    vmem = pl.BlockSpec(memory_space=pltpu.VMEM)
    return pl.pallas_call(
        solve_kernel,
        out_shape=(
            jax.ShapeDtypeStruct((ROUNDS, piv, piv), F32),
            jax.ShapeDtypeStruct((piv, piv), BF16),
            jax.ShapeDtypeStruct((8, piv), F32),
        ),
        in_specs=[vmem, vmem],
        out_specs=(vmem, vmem, vmem),
        scratch_shapes=[pltpu.VMEM((piv, piv), F32), pltpu.VMEM((piv, piv), F32)],
        compiler_params=pltpu.CompilerParams(vmem_limit_bytes=24 * 1024 * 1024),
        cost_estimate=pl.CostEstimate(flops=64 * 10**9, bytes_accessed=2 * 10**6, transcendentals=0),
        name="solve_pivots",
    )(x, l)


def apply_kernel(t_ref, tl_ref, x_ref, l_ref, inv_ref, ext_ref, sq_ref, col_ref, left_ref):
    width = t_ref.shape[1]
    piv = x_ref.shape[1]
    x = t_ref[...]
    wide = x.astype(F32)
    sq = jnp.sum(wide * wide, axis=1, keepdims=True)
    tl = tl_ref[...]
    cross = closeness(dot_nt(x, x_ref[0]), sq, sq_ref[0:1, :], width) - dot_nt(tl, l_ref[0])
    new0 = dot_nt_high(cross, inv_ref[0]).astype(BF16)
    cross = closeness(dot_nt(x, x_ref[1]), sq, sq_ref[1:2, :], width) - dot_nt(tl, l_ref[1]) - dot_nt(
        new0, ext_ref[...]
    )
    new1 = dot_nt_high(cross, inv_ref[1]).astype(BF16)
    col_ref[:, :piv] = new0
    col_ref[:, piv:] = new1
    total = jnp.zeros((x.shape[0], 128), F32)
    for part in (tl, new0, new1):
        part = part.astype(F32)
        part = part * part
        for t in range(part.shape[1] // 128):
            total = total + part[:, t * 128:(t + 1) * 128]
    turned = jnp.transpose(total)
    left_ref[...] = 1.0 - jnp.sum(turned, axis=0, keepdims=True)


def apply_all(features, factors, x, l, inv, ext, sq):
    rows, width = features.shape
    rank = factors.shape[1]
    piv = x.shape[1]
    tile = 256
    vmem = pl.BlockSpec(memory_space=pltpu.VMEM)
    return pl.pallas_call(
        apply_kernel,
        grid=(rows // tile,),
        out_shape=(
            jax.ShapeDtypeStruct((rows, ROUNDS * piv), BF16),
            jax.ShapeDtypeStruct((1, rows), F32),
        ),
        in_specs=[
            pl.BlockSpec((tile, width), lambda i: (i, 0)),
            pl.BlockSpec((tile, rank), lambda i: (i, 0)),
            vmem, vmem, vmem, vmem, vmem,
        ],
        out_specs=(
            pl.BlockSpec((tile, ROUNDS * piv), lambda i: (i, 0)),
            pl.BlockSpec((1, tile), lambda i: (0, i)),
        ),
        compiler_params=pltpu.CompilerParams(vmem_limit_bytes=32 * 1024 * 1024),
        cost_estimate=pl.CostEstimate(flops=3 * 10**9, bytes_accessed=8 * 10**6, transcendentals=0),
        name="apply_pivots",
    )(features, factors, x, l, inv, ext, sq)


PIECES = 4


def spread_kernel(size, feat_ref, fact_ref, piv_ref, own_ref, out_ref, g_ref, s1_ref, s2_ref, s3_ref,
                  r0_ref, r1_ref, r2_ref, up_ref, dn_ref, send_ref, send_sem, recv_sem):
    blk, grp = lax.axis_index("blk"), lax.axis_index("grp")
    core, xpos = lax.rem(grp, 2), lax.div(grp, 2)
    ypos, zpos = lax.rem(blk, 2), lax.div(blk, 2)
    last = size // 2 - 1
    mesh = pl.DeviceIdType.MESH
    near_core = (blk, grp + 1 - 2 * core)
    near_x = (blk, grp + 2 - 4 * xpos)
    near_y = (blk + 1 - 2 * ypos, grp)
    above = (lax.rem(blk + 2, size), grp)
    below = (lax.rem(blk + size - 2, size), grp)

    barrier = pltpu.get_barrier_semaphore()
    for other in (near_core, near_x, near_y, above, below):
        pl.semaphore_signal(barrier, inc=1, device_id=other, device_id_type=mesh)

    rows, width = feat_ref.shape
    rank = fact_ref.shape[1]
    piv = piv_ref.shape[1]
    me = blk * lax.axis_size("grp") + grp
    ids = lax.broadcasted_iota(jnp.int32, (rows, piv), 0)

    def gather(rnd):
        mine = jnp.where(own_ref[rnd] == me, 1.0, 0.0)
        pick = jnp.where(ids == piv_ref[rnd:rnd + 1, :], mine, 0.0).astype(BF16)
        g_ref[rnd, :, :width] = lax.dot_general(pick, feat_ref[...], TN, preferred_element_type=F32).astype(BF16)
        g_ref[rnd, :, width:] = lax.dot_general(pick, fact_ref[...], TN, preferred_element_type=F32).astype(BF16)

    per = PIECES // ROUNDS
    span = (width + rank) // per
    half, quarter, eighth = piv // 2, piv // 4, piv // 8

    class Piece:
        def __init__(self, p):
            self.p, self.rnd = p, p // per
            self.cols = pl.ds((p % per) * span, span)
            self.one, self.two = ((xpos, near_x), (ypos, near_y)) if p % 2 == 0 else ((ypos, near_y), (xpos, near_x))
            self.base1 = core * half
            self.base2 = self.base1 + self.one[0] * quarter
            self.base3 = self.base2 + self.two[0] * eighth

        def copy(self, k, src, dst, device):
            return pltpu.make_async_remote_copy(
                src_ref=src, dst_ref=dst, send_sem=send_sem.at[self.p, k], recv_sem=recv_sem.at[self.p, k],
                device_id=device, device_id_type=mesh)

        def out(self, base, count):
            return out_ref.at[self.rnd, pl.ds(pl.multiple_of(base, 16), count), self.cols]

        def link(self, k):
            p = self.p
            if k == 0:
                src = g_ref.at[self.rnd, pl.ds(pl.multiple_of((1 - core) * half, 16), half), self.cols]
                return self.copy(0, src, r0_ref.at[p], near_core)
            if k == 1:
                src = s1_ref.at[p, pl.ds(pl.multiple_of((1 - self.one[0]) * quarter, 16), quarter)]
                return self.copy(1, src, r1_ref.at[p], self.one[1])
            if k == 2:
                src = s2_ref.at[p, pl.ds(pl.multiple_of((1 - self.two[0]) * eighth, 16), eighth)]
                return self.copy(2, src, r2_ref.at[p], self.two[1])
            if k == 3:
                return self.copy(3, send_ref.at[p, 0], up_ref.at[p], above)
            if k == 4:
                return self.copy(4, send_ref.at[p, 1], dn_ref.at[p], below)
            if k == 5:
                return self.copy(5, self.out(self.base3, eighth), self.out(self.base3, eighth), self.two[1])
            if k == 6:
                return self.copy(6, self.out(self.base2, quarter), self.out(self.base2, quarter), self.one[1])
            return self.copy(7, self.out(self.base1, half), self.out(self.base1, half), near_core)

        def step(self, t):
            p = self.p
            if t == 0:
                self.link(0).start()
            elif t == 1:
                self.link(0).wait_recv()
                rows0 = pl.ds(pl.multiple_of(core * half, 16), half)
                s1_ref[p] = g_ref[self.rnd, rows0, self.cols] + r0_ref[p]
                self.link(1).start()
            elif t == 2:
                self.link(1).wait_recv()
                rows1 = pl.ds(pl.multiple_of(self.one[0] * quarter, 16), quarter)
                s2_ref[p] = s1_ref[p, rows1] + r1_ref[p]
                self.link(2).start()
            elif t == 3:
                self.link(2).wait_recv()
                rows2 = pl.ds(pl.multiple_of(self.two[0] * eighth, 16), eighth)
                s3_ref[p] = s2_ref[p, rows2] + r2_ref[p]

                @pl.when(zpos == 0)
                def _():
                    up_ref[p] = jnp.zeros_like(up_ref[p])
                    send_ref[p, 0] = s3_ref[p]
                    self.link(3).start()

                @pl.when(zpos == last)
                def _():
                    dn_ref[p] = jnp.zeros_like(dn_ref[p])
                    send_ref[p, 1] = s3_ref[p]
                    self.link(4).start()
            elif t == 4:
                def go_up():
                    @pl.when(zpos > 0)
                    def _():
                        self.link(3).wait_recv()

                    @pl.when((zpos > 0) & (zpos < last))
                    def _():
                        send_ref[p, 0] = s3_ref[p] + up_ref[p]
                        self.link(3).start()

                def go_down():
                    @pl.when(zpos < last)
                    def _():
                        self.link(4).wait_recv()

                    @pl.when((zpos > 0) & (zpos < last))
                    def _():
                        send_ref[p, 1] = s3_ref[p] + dn_ref[p]
                        self.link(4).start()

                @pl.when(2 * zpos <= last)
                def _():
                    go_up()
                    go_down()

                @pl.when(2 * zpos > last)
                def _():
                    go_down()
                    go_up()

                rows3 = pl.ds(pl.multiple_of(self.base3, 16), eighth)
                out_ref[self.rnd, rows3, self.cols] = s3_ref[p] + up_ref[p] + dn_ref[p]
                self.link(5).start()
            elif t == 5:
                self.link(5).wait_recv()
                self.link(6).start()
            elif t == 6:
                self.link(6).wait_recv()
                self.link(7).start()
            else:
                self.link(7).wait_recv()
                for k in (0, 1, 2, 5, 6, 7):
                    self.link(k).wait_send()

                @pl.when(zpos < last)
                def _():
                    self.link(3).wait_send()

                @pl.when(zpos > 0)
                def _():
                    self.link(4).wait_send()

    gather(0)
    pl.semaphore_wait(barrier, 5)
    pieces = [Piece(p) for p in range(PIECES)]
    for t in range(8 + PIECES - 1):
        for p in range(PIECES):
            if 0 <= t - p < 8:
                pieces[p].step(t - p)
            if p == 0 and t == 0:
                gather(1)


def spread_pivots(features, factors, pivots, owners):
    size = lax.axis_size("blk")
    piv = pivots.shape[1]
    width = features.shape[1] + factors.shape[1]
    span = width // (PIECES // ROUNDS)
    vmem = pl.BlockSpec(memory_space=pltpu.VMEM)
    buffer = lambda rows: pltpu.VMEM((PIECES, rows, span), BF16)
    return pl.pallas_call(
        functools.partial(spread_kernel, size),
        out_shape=jax.ShapeDtypeStruct((ROUNDS, piv, width), BF16),
        in_specs=[vmem, vmem, vmem, pl.BlockSpec(memory_space=pltpu.SMEM)],
        out_specs=vmem,
        scratch_shapes=[
            pltpu.VMEM((ROUNDS, piv, width), BF16),
            buffer(piv // 2), buffer(piv // 4), buffer(piv // 8),
            buffer(piv // 2), buffer(piv // 4), buffer(piv // 8),
            buffer(piv // 8), buffer(piv // 8),
            pltpu.VMEM((PIECES, 2, piv // 8, span), BF16),
            pltpu.SemaphoreType.DMA((PIECES, 8)),
            pltpu.SemaphoreType.DMA((PIECES, 8)),
        ],
        compiler_params=pltpu.CompilerParams(
            vmem_limit_bytes=40 * 1024 * 1024, collective_id=0, has_side_effects=True
        ),
        cost_estimate=pl.CostEstimate(flops=40 * 10**9, bytes_accessed=6 * 10**6, transcendentals=0),
        name="spread_pivots",
    )(features, factors, pivots, owners)


def squares(block):
    wide = block.astype(F32)
    return jnp.sum(wide * wide, axis=1)


def kernel_sum(left, right, left_sq):
    gram = jnp.dot(left, right.T, preferred_element_type=F32)
    dist = left_sq[:, None] + squares(right)[None, :] - 2.0 * gram
    return jnp.sum(jnp.exp(-dist / (8.0 * left.shape[1])), axis=1)


def on_device(features, factors, pivots, owners):
    rows = features.shape[0]
    count = lax.axis_size("blk")
    width = features.shape[1]
    spread = spread_pivots(features, factors, pivots, owners)
    x, l = spread[:, :, :width], spread[:, :, width:]

    odd = lax.axis_index("blk") % 2 == 1
    two_on = [(b, (b + 2) % count) for b in range(count)]
    swap = [(b, b ^ 1) for b in range(count)]
    chunks = 4
    size = rows // chunks
    own_sq = squares(features)
    total = kernel_sum(features, features, own_sq)
    for c in range(chunks):
        piece = lax.slice_in_dim(features, c * size, (c + 1) * size)
        second = lax.ppermute(piece, "blk", two_on)
        first = lax.ppermute(jnp.where(odd, second, piece), "blk", swap)
        total = total + kernel_sum(features, second, own_sq) + kernel_sum(features, first, own_sq)
    embedding = total / (3.0 * rows)

    inv, ext, sq = solve_pivots(x, l)
    columns, leftover = apply_all(features, factors, x, l, inv, ext, sq)
    return embedding, columns, leftover.reshape(rows)


def solution(mesh):
    placed = (P(("blk", "grp"), None), P(("blk", "grp"), None), P(), P())
    return jax.shard_map(
        on_device,
        mesh=mesh,
        in_specs=placed,
        out_specs=(P(("blk", "grp")), P(("blk", "grp"), None), P(("blk", "grp"))),
        check_vma=False,
    )
```

```python
import functools

import jax
import jax.numpy as jnp
from jax import lax
from jax.experimental import pallas as pl
from jax.experimental.pallas import tpu as pltpu
from jax.sharding import PartitionSpec as P

ROUNDS = 2
F32 = jnp.float32
BF16 = jnp.bfloat16
HIGHEST = lax.Precision.HIGHEST
VMEM_LIMIT = 56 * 1024 * 1024
NT = (((1,), (1,)), ((), ()))
TN = (((0,), (0,)), ((), ()))


def dot_nt(a, b):
    return lax.dot_general(a, b, NT, preferred_element_type=F32)


def dot_nt_high(a, b):
    return lax.dot_general(a, b, NT, precision=HIGHEST, preferred_element_type=F32)


def split3(x):
    high = x.astype(BF16).astype(F32)
    rest = x - high
    mid = rest.astype(BF16).astype(F32)
    return high, mid, rest - mid


def factor_start(m_ref, inv_ref):
    n = m_ref.shape[0]
    row = lax.broadcasted_iota(jnp.int32, (n, n), 0)
    col = lax.broadcasted_iota(jnp.int32, (n, n), 1)
    m_ref[...] = (row == col).astype(F32)
    inv_ref[...] = jnp.zeros((n, n), F32)


def factor_part(part, a_ref, m_ref, inv_ref):
    n = a_ref.shape[0]
    half = 128
    sub = lax.broadcasted_iota(jnp.int32, (8, 128), 0)

    left = part * half
    right = left + half
    wide = n - left
    lane = lax.broadcasted_iota(jnp.int32, (8, half), 1)

    def panel(k, carry):
        base = pl.multiple_of(left + k * 8, 8)
        rows = pl.ds(base, 8)
        panel_a = a_ref[rows, left:]
        panel_m = m_ref[rows, :right]
        diag = panel_a[:, :half]
        tiles = [panel_a[:, t * 128:(t + 1) * 128] for t in range(wide // 128)]
        tiles += [panel_m[:, t * 128:(t + 1) * 128] for t in range(right // 128)]
        cols = []
        for j in range(8):
            picked = jnp.where(lane == k * 8 + j, diag, 0.0)
            cols.append(jnp.broadcast_to(jnp.sum(picked, axis=1, keepdims=True), (8, 128)))
        scale = jnp.ones((8, 128), F32)
        for j in range(8):
            pivot = jnp.broadcast_to(cols[j][j:j + 1, :], (8, 128))
            scale = jnp.where(sub == j, pivot, scale)
            if j < 7:
                mult = jnp.where(sub > j, cols[j] / pivot, 0.0)
                for c in range(j + 1, 8):
                    cols[c] = cols[c] - mult * jnp.broadcast_to(cols[c][j:j + 1, :], (8, 128))
                tiles = [t - mult * jnp.broadcast_to(t[j:j + 1, :], (8, 128)) for t in tiles]
        scale = lax.rsqrt(scale)
        tiles = [t * scale for t in tiles]
        q = jnp.concatenate(tiles, axis=1)
        inv_ref[rows, :right] = q[:, wide:]
        h, m, l = split3(q)
        rhs = jnp.concatenate([h, m, h, l, h, m], axis=0).astype(BF16)
        lhs = jnp.concatenate([h, h, m, h, l, m], axis=0)[:, :wide].astype(BF16)
        upd = lax.dot_general(lhs, rhs, TN, preferred_element_type=F32)
        a_ref[left:, left:] = a_ref[left:, left:] - upd[:, :wide]
        m_ref[left:, :right] = m_ref[left:, :right] - upd[:, wide:]
        return carry

    lax.fori_loop(0, half // 8, panel, 0)


def diagonals(gram):
    n = gram.shape[0]
    row = lax.broadcasted_iota(jnp.int32, (n, n), 0)
    col = lax.broadcasted_iota(jnp.int32, (n, n), 1)
    only = jnp.where(row == col, gram, 0.0)
    return jnp.sum(only, axis=1, keepdims=True), jnp.sum(only, axis=0, keepdims=True)


def closeness(gram, left_sq, right_sq, width):
    return jnp.exp((2.0 * gram - left_sq - right_sq) / (8.0 * width))


PIECES = 4
CHUNKS = 12


def folded(x):
    total = None
    for t in range(x.shape[1] // 128):
        wide = x[:, t * 128:(t + 1) * 128].astype(F32)
        total = wide * wide if total is None else total + wide * wide
    return total


def row_sums(lanes):
    return jnp.sum(jnp.transpose(lanes), axis=0, keepdims=True)


def whole_kernel(size, feat_hbm, fact_hbm, piv_ref, own_ref, emb_ref, col_ref, left_ref,
                 feat_ref, fact_ref, second_ref, first_ref, acc_ref, sq_ref, out_ref, g_ref, s1_ref, s2_ref, s3_ref,
                 r0_ref, r1_ref, r2_ref, up_ref, dn_ref, send_ref, a_ref, m_ref, inv_ref, ext_ref,
                 send_sem, recv_sem, load_sem, zsend_sem, zrecv_sem, ysend_sem, yrecv_sem):
    blk, grp = lax.axis_index("blk"), lax.axis_index("grp")
    core, xpos = lax.rem(grp, 2), lax.div(grp, 2)
    ypos, zpos = lax.rem(blk, 2), lax.div(blk, 2)
    last = size // 2 - 1
    mesh = pl.DeviceIdType.MESH
    near_core = (blk, grp + 1 - 2 * core)
    near_x = (blk, grp + 2 - 4 * xpos)
    near_y = (blk + 1 - 2 * ypos, grp)
    above = (lax.rem(blk + 2, size), grp)
    below = (lax.rem(blk + size - 2, size), grp)

    load_x = pltpu.make_async_copy(feat_hbm, feat_ref, load_sem.at[0])
    load_l = pltpu.make_async_copy(fact_hbm, fact_ref, load_sem.at[1])
    load_x.start()
    load_l.start()

    barrier = pltpu.get_barrier_semaphore()
    for other in (near_core, near_x, near_y, above, below):
        pl.semaphore_signal(barrier, inc=1, device_id=other, device_id_type=mesh)

    rows, width = feat_ref.shape
    rank = fact_ref.shape[1]
    piv = piv_ref.shape[1]
    me = blk * lax.axis_size("grp") + grp
    ids = lax.broadcasted_iota(jnp.int32, (rows, piv), 0)

    def gather(rnd):
        mine = jnp.where(own_ref[rnd] == me, 1.0, 0.0)
        pick = jnp.where(ids == piv_ref[rnd:rnd + 1, :], mine, 0.0).astype(BF16)
        g_ref[rnd, :, :width] = lax.dot_general(pick, feat_ref[...], TN, preferred_element_type=F32).astype(BF16)
        g_ref[rnd, :, width:] = lax.dot_general(pick, fact_ref[...], TN, preferred_element_type=F32).astype(BF16)

    per = PIECES // ROUNDS
    span = (width + rank) // per
    half, quarter, eighth = piv // 2, piv // 4, piv // 8

    class Piece:
        def __init__(self, p):
            self.p, self.rnd = p, p // per
            self.cols = pl.ds((p % per) * span, span)
            self.one, self.two = ((xpos, near_x), (ypos, near_y)) if p % 2 == 0 else ((ypos, near_y), (xpos, near_x))
            self.base1 = core * half
            self.base2 = self.base1 + self.one[0] * quarter
            self.base3 = self.base2 + self.two[0] * eighth

        def copy(self, k, src, dst, device):
            return pltpu.make_async_remote_copy(
                src_ref=src, dst_ref=dst, send_sem=send_sem.at[self.p, k], recv_sem=recv_sem.at[self.p, k],
                device_id=device, device_id_type=mesh)

        def out(self, base, count):
            return out_ref.at[self.rnd, pl.ds(pl.multiple_of(base, 16), count), self.cols]

        def link(self, k):
            p = self.p
            if k == 0:
                src = g_ref.at[self.rnd, pl.ds(pl.multiple_of((1 - core) * half, 16), half), self.cols]
                return self.copy(0, src, r0_ref.at[p], near_core)
            if k == 1:
                src = s1_ref.at[p, pl.ds(pl.multiple_of((1 - self.one[0]) * quarter, 16), quarter)]
                return self.copy(1, src, r1_ref.at[p], self.one[1])
            if k == 2:
                src = s2_ref.at[p, pl.ds(pl.multiple_of((1 - self.two[0]) * eighth, 16), eighth)]
                return self.copy(2, src, r2_ref.at[p], self.two[1])
            if k == 3:
                return self.copy(3, send_ref.at[p, 0], up_ref.at[p], above)
            if k == 4:
                return self.copy(4, send_ref.at[p, 1], dn_ref.at[p], below)
            if k == 5:
                return self.copy(5, self.out(self.base3, eighth), self.out(self.base3, eighth), self.two[1])
            if k == 6:
                return self.copy(6, self.out(self.base2, quarter), self.out(self.base2, quarter), self.one[1])
            return self.copy(7, self.out(self.base1, half), self.out(self.base1, half), near_core)

        def step(self, t):
            p = self.p
            if t == 0:
                self.link(0).start()
            elif t == 1:
                self.link(0).wait_recv()
                rows0 = pl.ds(pl.multiple_of(core * half, 16), half)
                s1_ref[p] = g_ref[self.rnd, rows0, self.cols] + r0_ref[p]
                self.link(1).start()
            elif t == 2:
                self.link(1).wait_recv()
                rows1 = pl.ds(pl.multiple_of(self.one[0] * quarter, 16), quarter)
                s2_ref[p] = s1_ref[p, rows1] + r1_ref[p]
                self.link(2).start()
            elif t == 3:
                self.link(2).wait_recv()
                rows2 = pl.ds(pl.multiple_of(self.two[0] * eighth, 16), eighth)
                s3_ref[p] = s2_ref[p, rows2] + r2_ref[p]

                @pl.when(zpos == 0)
                def _():
                    up_ref[p] = jnp.zeros_like(up_ref[p])
                    send_ref[p, 0] = s3_ref[p]
                    self.link(3).start()

                @pl.when(zpos == last)
                def _():
                    dn_ref[p] = jnp.zeros_like(dn_ref[p])
                    send_ref[p, 1] = s3_ref[p]
                    self.link(4).start()
            elif t == 4:
                def go_up():
                    @pl.when(zpos > 0)
                    def _():
                        self.link(3).wait_recv()

                    @pl.when((zpos > 0) & (zpos < last))
                    def _():
                        send_ref[p, 0] = s3_ref[p] + up_ref[p]
                        self.link(3).start()

                def go_down():
                    @pl.when(zpos < last)
                    def _():
                        self.link(4).wait_recv()

                    @pl.when((zpos > 0) & (zpos < last))
                    def _():
                        send_ref[p, 1] = s3_ref[p] + dn_ref[p]
                        self.link(4).start()

                @pl.when(2 * zpos <= last)
                def _():
                    go_up()
                    go_down()

                @pl.when(2 * zpos > last)
                def _():
                    go_down()
                    go_up()

                rows3 = pl.ds(pl.multiple_of(self.base3, 16), eighth)
                out_ref[self.rnd, rows3, self.cols] = s3_ref[p] + up_ref[p] + dn_ref[p]
                self.link(5).start()
            elif t == 5:
                self.link(5).wait_recv()
                self.link(6).start()
            elif t == 6:
                self.link(6).wait_recv()
                self.link(7).start()
            else:
                self.link(7).wait_recv()
                for k in (0, 1, 2, 5, 6, 7):
                    self.link(k).wait_send()

                @pl.when(zpos < last)
                def _():
                    self.link(3).wait_send()

                @pl.when(zpos > 0)
                def _():
                    self.link(4).wait_send()

    chunk = rows // CHUNKS

    def part_of(ref, c):
        return ref.at[pl.ds(c * chunk, chunk)]

    def ahead(c):
        return pltpu.make_async_remote_copy(
            src_ref=part_of(feat_hbm, c), dst_ref=part_of(second_ref, c), send_sem=zsend_sem.at[c],
            recv_sem=zrecv_sem.at[c], device_id=above, device_id_type=mesh)

    def across(c, ref):
        return pltpu.make_async_remote_copy(
            src_ref=part_of(ref, c), dst_ref=part_of(first_ref, c), send_sem=ysend_sem.at[c],
            recv_sem=yrecv_sem.at[c], device_id=near_y, device_id_type=mesh)

    def relay(c):
        if not 0 <= c < CHUNKS:
            return

        @pl.when(ypos == 1)
        def _():
            ahead(c).wait_recv()
            across(c, second_ref).start()

        @pl.when(ypos == 0)
        def _():
            across(c, feat_ref).start()

    tile = 256
    tiles = rows // tile

    def embed(other_ref, i):
        part = other_ref[pl.ds(i * tile, tile), :]
        e = closeness(dot_nt(feat_ref[...], part), sq_ref[...], row_sums(folded(part)), width)
        for t in range(tile // 128):
            acc_ref[...] += e[:, t * 128:(t + 1) * 128]

    def embed_all(other_ref):
        def one(i, carry):
            embed(other_ref, i)
            return carry

        lax.fori_loop(0, tiles, one, 0)

    def start_own():
        acc_ref[...] = jnp.zeros_like(acc_ref)
        sq_ref[...] = jnp.sum(folded(feat_ref[...]), axis=1, keepdims=True)

    px = [out_ref.at[r, :, :width] for r in range(ROUNDS)]
    plow = [out_ref.at[r, :, width:] for r in range(ROUNDS)]

    pieces = [Piece(p) for p in range(PIECES)]

    def spread(t):
        for p in range(PIECES):
            if 0 <= t - p < 8:
                pieces[p].step(t - p)

    load_x.wait()
    load_l.wait()
    gather(0)
    pl.semaphore_wait(barrier, 5)
    steps = 8 + PIECES - 1
    for t in range(steps - 2):
        spread(t)
        ahead(t).start()
        relay(t - 3)
        if t == 0:
            gather(1)
        elif t == 1:
            start_own()
        elif t in (2, 3, 4):
            embed(feat_ref, t - 2)

    for c in range(steps - 2, CHUNKS):
        ahead(c).start()
    sent = steps - 5
    gram0 = dot_nt(px[0][...], px[0][...])
    c0, q0 = diagonals(gram0)
    a_ref[...] = closeness(gram0, c0, q0, width) - dot_nt(plow[0][...], plow[0][...])
    factor_start(m_ref, inv_ref.at[0])
    factor_part(0, a_ref, m_ref, inv_ref.at[0])
    spread(steps - 2)
    relay(sent)
    relay(sent + 1)
    factor_part(1, a_ref, m_ref, inv_ref.at[0])
    spread(steps - 1)
    relay(sent + 2)
    relay(sent + 3)
    gram1 = dot_nt(px[1][...], px[1][...])
    c1, q1 = diagonals(gram1)
    cross = closeness(dot_nt(px[1][...], px[0][...]), c1, q0, width) - dot_nt(plow[1][...], plow[0][...])
    ext = dot_nt_high(cross, inv_ref[0]).astype(BF16)
    ext_ref[...] = ext
    a_ref[...] = closeness(gram1, c1, q1, width) - dot_nt(plow[1][...], plow[1][...]) - dot_nt(ext, ext)
    factor_start(m_ref, inv_ref.at[1])
    factor_part(0, a_ref, m_ref, inv_ref.at[1])
    relay(sent + 4)
    relay(sent + 5)
    factor_part(1, a_ref, m_ref, inv_ref.at[1])
    for c in range(sent + 6, CHUNKS):
        relay(c)

    def extend(i, carry):
        here = pl.ds(pl.multiple_of(i * tile, tile), tile)
        x, tl, sq = feat_ref[here, :], fact_ref[here, :], sq_ref[here, :]
        cross = closeness(dot_nt(x, px[0][...]), sq, q0, width) - dot_nt(tl, plow[0][...])
        new0 = dot_nt_high(cross, inv_ref[0]).astype(BF16)
        cross = closeness(dot_nt(x, px[1][...]), sq, q1, width) - dot_nt(tl, plow[1][...]) - dot_nt(
            new0, ext_ref[...]
        )
        new1 = dot_nt_high(cross, inv_ref[1]).astype(BF16)
        col_ref[here, :piv] = new0
        col_ref[here, piv:] = new1
        left_ref[:, here] = 1.0 - row_sums(folded(tl) + folded(new0) + folded(new1))
        return carry

    lax.fori_loop(0, tiles, extend, 0)

    @pl.when(ypos == 0)
    def _():
        for c in range(CHUNKS):
            ahead(c).wait_recv()

    embed_all(second_ref)
    for c in range(CHUNKS):
        across(c, feat_ref).wait_recv()
    embed_all(first_ref)
    emb_ref[...] = row_sums(acc_ref[...]) / (3.0 * rows)
    for c in range(CHUNKS):
        ahead(c).wait_send()
        across(c, feat_ref).wait_send()


def everything(features, factors, pivots, owners):
    size = lax.axis_size("blk")
    rows, feats = features.shape
    rank = factors.shape[1]
    piv = pivots.shape[1]
    width = feats + rank
    span = width // (PIECES // ROUNDS)
    vmem = pl.BlockSpec(memory_space=pltpu.VMEM)
    anywhere = pl.BlockSpec(memory_space=pl.ANY)
    buffer = lambda count: pltpu.VMEM((PIECES, count, span), BF16)
    copies = lambda *shape: pltpu.SemaphoreType.DMA(shape)
    return pl.pallas_call(
        functools.partial(whole_kernel, size),
        out_shape=(
            jax.ShapeDtypeStruct((1, rows), F32),
            jax.ShapeDtypeStruct((rows, ROUNDS * piv), BF16),
            jax.ShapeDtypeStruct((1, rows), F32),
        ),
        in_specs=[anywhere, anywhere, vmem, pl.BlockSpec(memory_space=pltpu.SMEM)],
        out_specs=(vmem, vmem, vmem),
        scratch_shapes=[
            pltpu.VMEM((rows, feats), BF16), pltpu.VMEM((rows, rank), BF16),
            pltpu.VMEM((rows, feats), BF16), pltpu.VMEM((rows, feats), BF16),
            pltpu.VMEM((rows, 128), F32), pltpu.VMEM((rows, 1), F32),
            pltpu.VMEM((ROUNDS, piv, width), BF16), pltpu.VMEM((ROUNDS, piv, width), BF16),
            buffer(piv // 2), buffer(piv // 4), buffer(piv // 8),
            buffer(piv // 2), buffer(piv // 4), buffer(piv // 8),
            buffer(piv // 8), buffer(piv // 8),
            pltpu.VMEM((PIECES, 2, piv // 8, span), BF16),
            pltpu.VMEM((piv, piv), F32), pltpu.VMEM((piv, piv), F32),
            pltpu.VMEM((ROUNDS, piv, piv), F32), pltpu.VMEM((piv, piv), BF16),
            copies(PIECES, 8), copies(PIECES, 8), copies(2),
            copies(CHUNKS), copies(CHUNKS), copies(CHUNKS), copies(CHUNKS),
        ],
        compiler_params=pltpu.CompilerParams(
            vmem_limit_bytes=VMEM_LIMIT, collective_id=0, has_side_effects=True
        ),
        cost_estimate=pl.CostEstimate(flops=12 * 10**9, bytes_accessed=6 * 10**6, transcendentals=0),
        name="everything",
    )(features, factors, pivots, owners)


def on_device(features, factors, pivots, owners):
    rows = features.shape[0]
    embedding, columns, leftover = everything(features, factors, pivots, owners)
    return embedding.reshape(rows), columns, leftover.reshape(rows)


def solution(mesh):
    placed = (P(("blk", "grp"), None), P(("blk", "grp"), None), P(), P())
    return jax.shard_map(
        on_device,
        mesh=mesh,
        in_specs=placed,
        out_specs=(P(("blk", "grp")), P(("blk", "grp"), None), P(("blk", "grp"))),
        check_vma=False,
    )
```

```python
import functools

import jax
import jax.numpy as jnp
from jax import lax
from jax.experimental import pallas as pl
from jax.experimental.pallas import tpu as pltpu
from jax.sharding import PartitionSpec as P

ROUNDS = 2
F32 = jnp.float32
BF16 = jnp.bfloat16
HIGHEST = lax.Precision.HIGHEST
VMEM_LIMIT = 56 * 1024 * 1024
NT = (((1,), (1,)), ((), ()))
TN = (((0,), (0,)), ((), ()))


def dot_nt(a, b):
    return lax.dot_general(a, b, NT, preferred_element_type=F32)


def dot_nt_high(a, b):
    return lax.dot_general(a, b, NT, precision=HIGHEST, preferred_element_type=F32)


def split3(x):
    high = x.astype(BF16).astype(F32)
    rest = x - high
    mid = rest.astype(BF16).astype(F32)
    return high, mid, rest - mid


def factor_start(m_ref, inv_ref):
    n = m_ref.shape[0]
    row = lax.broadcasted_iota(jnp.int32, (n, n), 0)
    col = lax.broadcasted_iota(jnp.int32, (n, n), 1)
    m_ref[...] = (row == col).astype(F32)
    inv_ref[...] = jnp.zeros((n, n), F32)


def factor_part(part, a_ref, m_ref, inv_ref):
    n = a_ref.shape[0]
    half = 128
    sub = lax.broadcasted_iota(jnp.int32, (8, 128), 0)

    left = part * half
    right = left + half
    wide = n - left
    lane = lax.broadcasted_iota(jnp.int32, (8, half), 1)

    def panel(k, carry):
        base = pl.multiple_of(left + k * 8, 8)
        rows = pl.ds(base, 8)
        panel_a = a_ref[rows, left:]
        panel_m = m_ref[rows, :right]
        diag = panel_a[:, :half]
        tiles = [panel_a[:, t * 128:(t + 1) * 128] for t in range(wide // 128)]
        tiles += [panel_m[:, t * 128:(t + 1) * 128] for t in range(right // 128)]
        cols = []
        for j in range(8):
            picked = jnp.where(lane == k * 8 + j, diag, 0.0)
            cols.append(jnp.broadcast_to(jnp.sum(picked, axis=1, keepdims=True), (8, 128)))
        scale = jnp.ones((8, 128), F32)
        for j in range(8):
            pivot = jnp.broadcast_to(cols[j][j:j + 1, :], (8, 128))
            scale = jnp.where(sub == j, pivot, scale)
            if j < 7:
                mult = jnp.where(sub > j, cols[j] / pivot, 0.0)
                for c in range(j + 1, 8):
                    cols[c] = cols[c] - mult * jnp.broadcast_to(cols[c][j:j + 1, :], (8, 128))
                tiles = [t - mult * jnp.broadcast_to(t[j:j + 1, :], (8, 128)) for t in tiles]
        scale = lax.rsqrt(scale)
        tiles = [t * scale for t in tiles]
        q = jnp.concatenate(tiles, axis=1)
        inv_ref[rows, :right] = q[:, wide:]
        h, m, l = split3(q)
        rhs = jnp.concatenate([h, m, h, l, h, m], axis=0).astype(BF16)
        lhs = jnp.concatenate([h, h, m, h, l, m], axis=0)[:, :wide].astype(BF16)
        upd = lax.dot_general(lhs, rhs, TN, preferred_element_type=F32)
        a_ref[left:, left:] = a_ref[left:, left:] - upd[:, :wide]
        m_ref[left:, :right] = m_ref[left:, :right] - upd[:, wide:]
        return carry

    lax.fori_loop(0, half // 8, panel, 0)


def diagonals(gram):
    n = gram.shape[0]
    row = lax.broadcasted_iota(jnp.int32, (n, n), 0)
    col = lax.broadcasted_iota(jnp.int32, (n, n), 1)
    only = jnp.where(row == col, gram, 0.0)
    return jnp.sum(only, axis=1, keepdims=True), jnp.sum(only, axis=0, keepdims=True)


def closeness(gram, left_sq, right_sq, width):
    return jnp.exp((2.0 * gram - left_sq - right_sq) / (8.0 * width))


PIECES = 4
CHUNKS = 12


def folded(x):
    total = None
    for t in range(x.shape[1] // 128):
        wide = x[:, t * 128:(t + 1) * 128].astype(F32)
        total = wide * wide if total is None else total + wide * wide
    return total


def row_sums(lanes):
    return jnp.sum(jnp.transpose(lanes), axis=0, keepdims=True)


def whole_kernel(size, feat_hbm, fact_hbm, piv_ref, own_ref, emb_ref, col_ref, left_ref,
                 feat_ref, fact_ref, second_ref, first_ref, acc_ref, sq_ref, out_ref, g_ref, s1_ref, s2_ref, s3_ref,
                 r0_ref, r1_ref, r2_ref, up_ref, dn_ref, send_ref, a_ref, m_ref, inv_ref, ext_ref, sums_ref,
                 send_sem, recv_sem, load_sem, zsend_sem, zrecv_sem, ysend_sem, yrecv_sem):
    blk, grp = lax.axis_index("blk"), lax.axis_index("grp")
    core, xpos = lax.rem(grp, 2), lax.div(grp, 2)
    ypos, zpos = lax.rem(blk, 2), lax.div(blk, 2)
    last = size // 2 - 1
    mesh = pl.DeviceIdType.MESH
    near_core = (blk, grp + 1 - 2 * core)
    near_x = (blk, grp + 2 - 4 * xpos)
    near_y = (blk + 1 - 2 * ypos, grp)
    above = (lax.rem(blk + 2, size), grp)
    below = (lax.rem(blk + size - 2, size), grp)

    load_x = pltpu.make_async_copy(feat_hbm, feat_ref, load_sem.at[0])
    load_l = pltpu.make_async_copy(fact_hbm, fact_ref, load_sem.at[1])
    load_x.start()
    load_l.start()

    barrier = pltpu.get_barrier_semaphore()
    for other in (near_core, near_x, near_y, above, below):
        pl.semaphore_signal(barrier, inc=1, device_id=other, device_id_type=mesh)

    rows, width = feat_ref.shape
    rank = fact_ref.shape[1]
    piv = piv_ref.shape[1]
    me = blk * lax.axis_size("grp") + grp
    ids = lax.broadcasted_iota(jnp.int32, (rows, piv), 0)

    def gather(rnd):
        mine = jnp.where(own_ref[rnd] == me, 1.0, 0.0)
        pick = jnp.where(ids == piv_ref[rnd:rnd + 1, :], mine, 0.0).astype(BF16)
        g_ref[rnd, :, :width] = lax.dot_general(pick, feat_ref[...], TN, preferred_element_type=F32).astype(BF16)
        g_ref[rnd, :, width:] = lax.dot_general(pick, fact_ref[...], TN, preferred_element_type=F32).astype(BF16)

    per = PIECES // ROUNDS
    span = (width + rank) // per
    half, quarter, eighth = piv // 2, piv // 4, piv // 8

    class Piece:
        def __init__(self, p):
            self.p, self.rnd = p, p // per
            self.cols = pl.ds((p % per) * span, span)
            self.one, self.two = (xpos, near_x), (ypos, near_y)
            self.base1 = core * half
            self.base2 = self.base1 + self.one[0] * quarter
            self.base3 = self.base2 + self.two[0] * eighth

        def copy(self, k, src, dst, device):
            return pltpu.make_async_remote_copy(
                src_ref=src, dst_ref=dst, send_sem=send_sem.at[self.p, k], recv_sem=recv_sem.at[self.p, k],
                device_id=device, device_id_type=mesh)

        def out(self, base, count):
            return out_ref.at[self.rnd, pl.ds(pl.multiple_of(base, 16), count), self.cols]

        def link(self, k):
            p = self.p
            if k == 0:
                src = g_ref.at[self.rnd, pl.ds(pl.multiple_of((1 - core) * half, 16), half), self.cols]
                return self.copy(0, src, r0_ref.at[p], near_core)
            if k == 1:
                src = s1_ref.at[p, pl.ds(pl.multiple_of((1 - self.one[0]) * quarter, 16), quarter)]
                return self.copy(1, src, r1_ref.at[p], self.one[1])
            if k == 2:
                src = s2_ref.at[p, pl.ds(pl.multiple_of((1 - self.two[0]) * eighth, 16), eighth)]
                return self.copy(2, src, r2_ref.at[p], self.two[1])
            if k == 3:
                return self.copy(3, send_ref.at[p, 0], up_ref.at[p], above)
            if k == 4:
                return self.copy(4, send_ref.at[p, 1], dn_ref.at[p], below)
            if k == 5:
                return self.copy(5, self.out(self.base3, eighth), self.out(self.base3, eighth), self.two[1])
            if k == 6:
                return self.copy(6, self.out(self.base2, quarter), self.out(self.base2, quarter), self.one[1])
            return self.copy(7, self.out(self.base1, half), self.out(self.base1, half), near_core)

        def step(self, t):
            p = self.p
            if t == 0:
                self.link(0).start()
            elif t == 1:
                self.link(0).wait_recv()
                rows0 = pl.ds(pl.multiple_of(core * half, 16), half)
                s1_ref[p] = g_ref[self.rnd, rows0, self.cols] + r0_ref[p]
                self.link(1).start()
            elif t == 2:
                self.link(1).wait_recv()
                rows1 = pl.ds(pl.multiple_of(self.one[0] * quarter, 16), quarter)
                s2_ref[p] = s1_ref[p, rows1] + r1_ref[p]
                self.link(2).start()
            elif t == 3:
                self.link(2).wait_recv()
                rows2 = pl.ds(pl.multiple_of(self.two[0] * eighth, 16), eighth)
                s3_ref[p] = s2_ref[p, rows2] + r2_ref[p]

                @pl.when(zpos == 0)
                def _():
                    up_ref[p] = jnp.zeros_like(up_ref[p])
                    send_ref[p, 0] = s3_ref[p]
                    self.link(3).start()

                @pl.when(zpos == last)
                def _():
                    dn_ref[p] = jnp.zeros_like(dn_ref[p])
                    send_ref[p, 1] = s3_ref[p]
                    self.link(4).start()
            elif t < 3 + last:
                hop = t - 3

                @pl.when(zpos == hop)
                def _():
                    self.link(3).wait_recv()
                    send_ref[p, 0] = s3_ref[p] + up_ref[p]
                    self.link(3).start()

                @pl.when(zpos == last - hop)
                def _():
                    self.link(4).wait_recv()
                    send_ref[p, 1] = s3_ref[p] + dn_ref[p]
                    self.link(4).start()
            elif t == 3 + last:
                @pl.when(zpos == last)
                def _():
                    self.link(3).wait_recv()

                @pl.when(zpos == 0)
                def _():
                    self.link(4).wait_recv()

                rows3 = pl.ds(pl.multiple_of(self.base3, 16), eighth)
                out_ref[self.rnd, rows3, self.cols] = s3_ref[p] + up_ref[p] + dn_ref[p]
                self.link(5).start()
            elif t == 4 + last:
                self.link(5).wait_recv()
                self.link(6).start()
            elif t == 5 + last:
                self.link(6).wait_recv()
                self.link(7).start()
            else:
                self.link(7).wait_recv()
                for k in (0, 1, 2, 5, 6, 7):
                    self.link(k).wait_send()

                @pl.when(zpos < last)
                def _():
                    self.link(3).wait_send()

                @pl.when(zpos > 0)
                def _():
                    self.link(4).wait_send()

    chunk = rows // CHUNKS

    def part_of(ref, c):
        return ref.at[pl.ds(c * chunk, chunk)]

    def ahead(c):
        return pltpu.make_async_remote_copy(
            src_ref=part_of(feat_hbm, c), dst_ref=part_of(second_ref, c), send_sem=zsend_sem.at[c],
            recv_sem=zrecv_sem.at[c], device_id=above, device_id_type=mesh)

    def across(c, ref):
        return pltpu.make_async_remote_copy(
            src_ref=part_of(ref, c), dst_ref=part_of(first_ref, c), send_sem=ysend_sem.at[c],
            recv_sem=yrecv_sem.at[c], device_id=near_y, device_id_type=mesh)

    def relay(c):
        if not 0 <= c < CHUNKS:
            return

        @pl.when(ypos == 1)
        def _():
            ahead(c).wait_recv()
            across(c, second_ref).start()

        @pl.when(ypos == 0)
        def _():
            across(c, feat_ref).start()

    tile = 256
    tiles = rows // tile

    def embed(other_ref, i):
        part = other_ref[pl.ds(i * tile, tile), :]
        e = closeness(dot_nt(feat_ref[...], part), sq_ref[...], row_sums(folded(part)), width)
        for t in range(tile // 128):
            acc_ref[...] += e[:, t * 128:(t + 1) * 128]

    def embed_all(other_ref):
        def one(i, carry):
            embed(other_ref, i)
            return carry

        lax.fori_loop(0, tiles, one, 0)

    def start_own():
        acc_ref[...] = jnp.zeros_like(acc_ref)
        sq_ref[...] = jnp.sum(folded(feat_ref[...]), axis=1, keepdims=True)

    px = [out_ref.at[r, :, :width] for r in range(ROUNDS)]
    plow = [out_ref.at[r, :, width:] for r in range(ROUNDS)]

    pieces = [Piece(p) for p in range(PIECES)]
    length = 7 + last

    def spread(t):
        for p in range(PIECES):
            if 0 <= t - p < length:
                pieces[p].step(t - p)

    load_x.wait()
    load_l.wait()
    gather(0)
    pl.semaphore_wait(barrier, 5)
    steps = length + PIECES - 1
    started = 0
    relayed = 0
    for t in range(steps - 2):
        spread(t)

        @pl.when(zpos == last)
        def _():
            for c in range(3 * t, min(3 * t + 3, CHUNKS)):
                ahead(c).start()

        if t < CHUNKS:
            @pl.when(zpos < last)
            def _():
                ahead(t).start()

            started = t + 1
        if t % 2 == 0 and 2 <= t < 12:
            relay(t // 2 - 1)
            relayed = t // 2
        if t == 0:
            gather(1)
        elif t == 1:
            start_own()
        elif t in (2, 3, 4):
            embed(feat_ref, t - 2)

    @pl.when(zpos < last)
    def _():
        for c in range(started, CHUNKS):
            ahead(c).start()

    gram0 = dot_nt(px[0][...], px[0][...])
    c0, q0 = diagonals(gram0)
    a_ref[...] = closeness(gram0, c0, q0, width) - dot_nt(plow[0][...], plow[0][...])
    factor_start(m_ref, inv_ref.at[0])
    factor_part(0, a_ref, m_ref, inv_ref.at[0])
    spread(steps - 2)
    relay(relayed)
    factor_part(1, a_ref, m_ref, inv_ref.at[0])
    spread(steps - 1)
    relay(relayed + 1)
    relay(relayed + 2)
    gram1 = dot_nt(px[1][...], px[1][...])
    c1, q1 = diagonals(gram1)
    cross = closeness(dot_nt(px[1][...], px[0][...]), c1, q0, width) - dot_nt(plow[1][...], plow[0][...])
    ext = dot_nt_high(cross, inv_ref[0]).astype(BF16)
    ext_ref[...] = ext
    a_ref[...] = closeness(gram1, c1, q1, width) - dot_nt(plow[1][...], plow[1][...]) - dot_nt(ext, ext)
    factor_start(m_ref, inv_ref.at[1])
    factor_part(0, a_ref, m_ref, inv_ref.at[1])
    relay(relayed + 3)
    relay(relayed + 4)
    factor_part(1, a_ref, m_ref, inv_ref.at[1])
    relay(relayed + 5)

    def extend(i, carry):
        here = pl.ds(pl.multiple_of(i * tile, tile), tile)
        x, tl, sq = feat_ref[here, :], fact_ref[here, :], sq_ref[here, :]
        cross = closeness(dot_nt(x, px[0][...]), sq, q0, width) - dot_nt(tl, plow[0][...])
        new0 = dot_nt_high(cross, inv_ref[0]).astype(BF16)
        cross = closeness(dot_nt(x, px[1][...]), sq, q1, width) - dot_nt(tl, plow[1][...]) - dot_nt(
            new0, ext_ref[...]
        )
        new1 = dot_nt_high(cross, inv_ref[1]).astype(BF16)
        col_ref[here, :piv] = new0
        col_ref[here, piv:] = new1
        sums_ref[:, here] = 1.0 - row_sums(folded(tl) + folded(new0) + folded(new1))
        return carry

    lax.fori_loop(0, tiles, extend, 0)
    for c in range(relayed + 6, CHUNKS):
        relay(c)

    @pl.when(ypos == 0)
    def _():
        for c in range(CHUNKS):
            ahead(c).wait_recv()

    embed_all(second_ref)
    for c in range(CHUNKS):
        across(c, feat_ref).wait_recv()
    embed_all(first_ref)
    means = row_sums(acc_ref[...]) / (3.0 * rows)
    left = sums_ref[...]
    for t in range(rows // 128):
        emb_ref[t:t + 1, :] = means[:, t * 128:(t + 1) * 128]
        left_ref[t:t + 1, :] = left[:, t * 128:(t + 1) * 128]
    for c in range(CHUNKS):
        ahead(c).wait_send()
        across(c, feat_ref).wait_send()


def everything(features, factors, pivots, owners):
    size = lax.axis_size("blk")
    rows, feats = features.shape
    rank = factors.shape[1]
    piv = pivots.shape[1]
    width = feats + rank
    span = width // (PIECES // ROUNDS)
    vmem = pl.BlockSpec(memory_space=pltpu.VMEM)
    anywhere = pl.BlockSpec(memory_space=pl.ANY)
    buffer = lambda count: pltpu.VMEM((PIECES, count, span), BF16)
    copies = lambda *shape: pltpu.SemaphoreType.DMA(shape)
    return pl.pallas_call(
        functools.partial(whole_kernel, size),
        out_shape=(
            jax.ShapeDtypeStruct((rows // 128, 128), F32),
            jax.ShapeDtypeStruct((rows, ROUNDS * piv), BF16),
            jax.ShapeDtypeStruct((rows // 128, 128), F32),
        ),
        in_specs=[anywhere, anywhere, vmem, pl.BlockSpec(memory_space=pltpu.SMEM)],
        out_specs=(vmem, vmem, vmem),
        scratch_shapes=[
            pltpu.VMEM((rows, feats), BF16), pltpu.VMEM((rows, rank), BF16),
            pltpu.VMEM((rows, feats), BF16), pltpu.VMEM((rows, feats), BF16),
            pltpu.VMEM((rows, 128), F32), pltpu.VMEM((rows, 1), F32),
            pltpu.VMEM((ROUNDS, piv, width), BF16), pltpu.VMEM((ROUNDS, piv, width), BF16),
            buffer(piv // 2), buffer(piv // 4), buffer(piv // 8),
            buffer(piv // 2), buffer(piv // 4), buffer(piv // 8),
            buffer(piv // 8), buffer(piv // 8),
            pltpu.VMEM((PIECES, 2, piv // 8, span), BF16),
            pltpu.VMEM((piv, piv), F32), pltpu.VMEM((piv, piv), F32),
            pltpu.VMEM((ROUNDS, piv, piv), F32), pltpu.VMEM((piv, piv), BF16), pltpu.VMEM((1, rows), F32),
            copies(PIECES, 8), copies(PIECES, 8), copies(2),
            copies(CHUNKS), copies(CHUNKS), copies(CHUNKS), copies(CHUNKS),
        ],
        compiler_params=pltpu.CompilerParams(
            vmem_limit_bytes=VMEM_LIMIT, collective_id=0, has_side_effects=True
        ),
        cost_estimate=pl.CostEstimate(flops=12 * 10**9, bytes_accessed=6 * 10**6, transcendentals=0),
        name="everything",
    )(features, factors, pivots, owners)


def on_device(features, factors, pivots, owners):
    rows = features.shape[0]
    embedding, columns, leftover = everything(features, factors, pivots, owners)
    return embedding.reshape(rows), columns, leftover.reshape(rows)


def solution(mesh):
    placed = (P(("blk", "grp"), None), P(("blk", "grp"), None), P(), P())
    return jax.shard_map(
        on_device,
        mesh=mesh,
        in_specs=placed,
        out_specs=(P(("blk", "grp")), P(("blk", "grp"), None), P(("blk", "grp"))),
        check_vma=False,
    )
```

```python
import functools

import jax
import jax.numpy as jnp
from jax import lax
from jax.experimental import pallas as pl
from jax.experimental.pallas import tpu as pltpu
from jax.sharding import PartitionSpec as P

ROUNDS = 2
F32 = jnp.float32
BF16 = jnp.bfloat16
HIGHEST = lax.Precision.HIGHEST
VMEM_LIMIT = 56 * 1024 * 1024
NT = (((1,), (1,)), ((), ()))
TN = (((0,), (0,)), ((), ()))


def dot_nt(a, b):
    return lax.dot_general(a, b, NT, preferred_element_type=F32)


def dot_nt_high(a, b):
    return lax.dot_general(a, b, NT, precision=HIGHEST, preferred_element_type=F32)


def split3(x):
    high = x.astype(BF16).astype(F32)
    rest = x - high
    mid = rest.astype(BF16).astype(F32)
    return high, mid, rest - mid


def factor_start(m_ref, inv_ref):
    n = m_ref.shape[0]
    row = lax.broadcasted_iota(jnp.int32, (n, n), 0)
    col = lax.broadcasted_iota(jnp.int32, (n, n), 1)
    m_ref[...] = (row == col).astype(F32)
    inv_ref[...] = jnp.zeros((n, n), F32)


def factor_part(part, a_ref, m_ref, inv_ref):
    n = a_ref.shape[0]
    half = 128
    sub = lax.broadcasted_iota(jnp.int32, (8, 128), 0)

    left = part * half
    right = left + half
    wide = n - left
    lane = lax.broadcasted_iota(jnp.int32, (8, half), 1)

    def panel(k, carry):
        base = pl.multiple_of(left + k * 8, 8)
        rows = pl.ds(base, 8)
        panel_a = a_ref[rows, left:]
        panel_m = m_ref[rows, :right]
        diag = panel_a[:, :half]
        tiles = [panel_a[:, t * 128:(t + 1) * 128] for t in range(wide // 128)]
        tiles += [panel_m[:, t * 128:(t + 1) * 128] for t in range(right // 128)]
        cols = []
        for j in range(8):
            picked = jnp.where(lane == k * 8 + j, diag, 0.0)
            cols.append(jnp.broadcast_to(jnp.sum(picked, axis=1, keepdims=True), (8, 128)))
        scale = jnp.ones((8, 128), F32)
        for j in range(8):
            pivot = jnp.broadcast_to(cols[j][j:j + 1, :], (8, 128))
            scale = jnp.where(sub == j, pivot, scale)
            if j < 7:
                mult = jnp.where(sub > j, cols[j] / pivot, 0.0)
                for c in range(j + 1, 8):
                    cols[c] = cols[c] - mult * jnp.broadcast_to(cols[c][j:j + 1, :], (8, 128))
                tiles = [t - mult * jnp.broadcast_to(t[j:j + 1, :], (8, 128)) for t in tiles]
        scale = lax.rsqrt(scale)
        tiles = [t * scale for t in tiles]
        q = jnp.concatenate(tiles, axis=1)
        inv_ref[rows, :right] = q[:, wide:]
        h, m, l = split3(q)
        rhs = jnp.concatenate([h, m, h, l, h, m], axis=0).astype(BF16)
        lhs = jnp.concatenate([h, h, m, h, l, m], axis=0)[:, :wide].astype(BF16)
        upd = lax.dot_general(lhs, rhs, TN, preferred_element_type=F32)
        a_ref[left:, left:] = a_ref[left:, left:] - upd[:, :wide]
        m_ref[left:, :right] = m_ref[left:, :right] - upd[:, wide:]
        return carry

    lax.fori_loop(0, half // 8, panel, 0)


def diagonals(gram):
    n = gram.shape[0]
    row = lax.broadcasted_iota(jnp.int32, (n, n), 0)
    col = lax.broadcasted_iota(jnp.int32, (n, n), 1)
    only = jnp.where(row == col, gram, 0.0)
    return jnp.sum(only, axis=1, keepdims=True), jnp.sum(only, axis=0, keepdims=True)


def closeness(gram, left_sq, right_sq, width):
    return jnp.exp((2.0 * gram - left_sq - right_sq) / (8.0 * width))


PIECES = 4
CHUNKS = 12


def folded(x):
    total = None
    for t in range(x.shape[1] // 128):
        wide = x[:, t * 128:(t + 1) * 128].astype(F32)
        total = wide * wide if total is None else total + wide * wide
    return total


def row_sums(lanes):
    return jnp.sum(jnp.transpose(lanes), axis=0, keepdims=True)


def whole_kernel(size, feat_hbm, fact_hbm, piv_ref, own_ref, emb_ref, col_ref, left_ref,
                 feat_ref, fact_ref, second_ref, first_ref, acc_ref, sq_ref, out_ref, g_ref, s1_ref, s2_ref, s3_ref,
                 r0_ref, r1_ref, r2_ref, up_ref, dn_ref, send_ref, a_ref, m_ref, inv_ref, ext_ref, sums_ref,
                 send_sem, recv_sem, load_sem, zsend_sem, zrecv_sem, ysend_sem, yrecv_sem):
    blk, grp = lax.axis_index("blk"), lax.axis_index("grp")
    core, xpos = lax.rem(grp, 2), lax.div(grp, 2)
    ypos, zpos = lax.rem(blk, 2), lax.div(blk, 2)
    last = size // 2 - 1
    mesh = pl.DeviceIdType.MESH
    near_core = (blk, grp + 1 - 2 * core)
    near_x = (blk, grp + 2 - 4 * xpos)
    near_y = (blk + 1 - 2 * ypos, grp)
    above = (lax.rem(blk + 2, size), grp)
    below = (lax.rem(blk + size - 2, size), grp)

    load_x = pltpu.make_async_copy(feat_hbm, feat_ref, load_sem.at[0])
    load_l = pltpu.make_async_copy(fact_hbm, fact_ref, load_sem.at[1])
    load_x.start()
    load_l.start()

    barrier = pltpu.get_barrier_semaphore()
    for other in (near_core, near_x, near_y, above, below):
        pl.semaphore_signal(barrier, inc=1, device_id=other, device_id_type=mesh)

    rows, width = feat_ref.shape
    rank = fact_ref.shape[1]
    piv = piv_ref.shape[1]
    me = blk * lax.axis_size("grp") + grp
    ids = lax.broadcasted_iota(jnp.int32, (rows, piv), 0)

    def gather(rnd):
        mine = jnp.where(own_ref[rnd] == me, 1.0, 0.0)
        pick = jnp.where(ids == piv_ref[rnd:rnd + 1, :], mine, 0.0).astype(BF16)
        g_ref[rnd, :, :width] = lax.dot_general(pick, feat_ref[...], TN, preferred_element_type=F32).astype(BF16)
        g_ref[rnd, :, width:] = lax.dot_general(pick, fact_ref[...], TN, preferred_element_type=F32).astype(BF16)

    per = PIECES // ROUNDS
    span = (width + rank) // per
    half, quarter, eighth = piv // 2, piv // 4, piv // 8

    class Piece:
        def __init__(self, p):
            self.p, self.rnd = p, p // per
            self.cols = pl.ds((p % per) * span, span)
            self.one, self.two = (xpos, near_x), (ypos, near_y)
            self.base1 = core * half
            self.base2 = self.base1 + self.one[0] * quarter
            self.base3 = self.base2 + self.two[0] * eighth

        def copy(self, k, src, dst, device):
            return pltpu.make_async_remote_copy(
                src_ref=src, dst_ref=dst, send_sem=send_sem.at[self.p, k], recv_sem=recv_sem.at[self.p, k],
                device_id=device, device_id_type=mesh)

        def out(self, base, count):
            return out_ref.at[self.rnd, pl.ds(pl.multiple_of(base, 16), count), self.cols]

        def link(self, k):
            p = self.p
            if k == 0:
                src = g_ref.at[self.rnd, pl.ds(pl.multiple_of((1 - core) * half, 16), half), self.cols]
                return self.copy(0, src, r0_ref.at[p], near_core)
            if k == 1:
                src = s1_ref.at[p, pl.ds(pl.multiple_of((1 - self.one[0]) * quarter, 16), quarter)]
                return self.copy(1, src, r1_ref.at[p], self.one[1])
            if k == 2:
                src = s2_ref.at[p, pl.ds(pl.multiple_of((1 - self.two[0]) * eighth, 16), eighth)]
                return self.copy(2, src, r2_ref.at[p], self.two[1])
            if k == 3:
                return self.copy(3, send_ref.at[p, 0], up_ref.at[p], above)
            if k == 4:
                return self.copy(4, send_ref.at[p, 1], dn_ref.at[p], below)
            if k == 5:
                return self.copy(5, self.out(self.base3, eighth), self.out(self.base3, eighth), self.two[1])
            if k == 6:
                return self.copy(6, self.out(self.base2, quarter), self.out(self.base2, quarter), self.one[1])
            return self.copy(7, self.out(self.base1, half), self.out(self.base1, half), near_core)

        def step(self, t):
            p = self.p
            if t == 0:
                self.link(0).start()
            elif t == 1:
                self.link(0).wait_recv()
                rows0 = pl.ds(pl.multiple_of(core * half, 16), half)
                s1_ref[p] = g_ref[self.rnd, rows0, self.cols] + r0_ref[p]
                self.link(1).start()
            elif t == 2:
                self.link(1).wait_recv()
                rows1 = pl.ds(pl.multiple_of(self.one[0] * quarter, 16), quarter)
                s2_ref[p] = s1_ref[p, rows1] + r1_ref[p]
                self.link(2).start()
            elif t == 3:
                self.link(2).wait_recv()
                rows2 = pl.ds(pl.multiple_of(self.two[0] * eighth, 16), eighth)
                s3_ref[p] = s2_ref[p, rows2] + r2_ref[p]

                @pl.when(zpos == 0)
                def _():
                    up_ref[p] = jnp.zeros_like(up_ref[p])
                    send_ref[p, 0] = s3_ref[p]
                    self.link(3).start()

                @pl.when(zpos == last)
                def _():
                    dn_ref[p] = jnp.zeros_like(dn_ref[p])
                    send_ref[p, 1] = s3_ref[p]
                    self.link(4).start()
            elif t < 3 + last:
                hop = t - 3

                @pl.when(zpos == hop)
                def _():
                    self.link(3).wait_recv()
                    send_ref[p, 0] = s3_ref[p] + up_ref[p]
                    self.link(3).start()

                @pl.when(zpos == last - hop)
                def _():
                    self.link(4).wait_recv()
                    send_ref[p, 1] = s3_ref[p] + dn_ref[p]
                    self.link(4).start()
            elif t == 3 + last:
                @pl.when(zpos == last)
                def _():
                    self.link(3).wait_recv()

                @pl.when(zpos == 0)
                def _():
                    self.link(4).wait_recv()

                rows3 = pl.ds(pl.multiple_of(self.base3, 16), eighth)
                out_ref[self.rnd, rows3, self.cols] = s3_ref[p] + up_ref[p] + dn_ref[p]
                self.link(5).start()
            elif t == 4 + last:
                self.link(5).wait_recv()
                self.link(6).start()
            elif t == 5 + last:
                self.link(6).wait_recv()
                self.link(7).start()
            else:
                self.link(7).wait_recv()
                for k in (0, 1, 2, 5, 6, 7):
                    self.link(k).wait_send()

                @pl.when(zpos < last)
                def _():
                    self.link(3).wait_send()

                @pl.when(zpos > 0)
                def _():
                    self.link(4).wait_send()

    chunk = rows // CHUNKS

    def part_of(ref, c):
        return ref.at[pl.ds(c * chunk, chunk)]

    def ahead(c):
        return pltpu.make_async_remote_copy(
            src_ref=part_of(feat_hbm, c), dst_ref=part_of(second_ref, c), send_sem=zsend_sem.at[c],
            recv_sem=zrecv_sem.at[c], device_id=above, device_id_type=mesh)

    def across(c, ref):
        return pltpu.make_async_remote_copy(
            src_ref=part_of(ref, c), dst_ref=part_of(first_ref, c), send_sem=ysend_sem.at[c],
            recv_sem=yrecv_sem.at[c], device_id=near_y, device_id_type=mesh)

    def relay(c):
        if not 0 <= c < CHUNKS:
            return

        @pl.when(ypos == 1)
        def _():
            ahead(c).wait_recv()
            across(c, second_ref).start()

        @pl.when(ypos == 0)
        def _():
            across(c, feat_ref).start()

    tile = 256
    tiles = rows // tile

    def embed(other_ref, i):
        part = other_ref[pl.ds(i * tile, tile), :]
        e = closeness(dot_nt(feat_ref[...], part), sq_ref[...], row_sums(folded(part)), width)
        for t in range(tile // 128):
            acc_ref[...] += e[:, t * 128:(t + 1) * 128]

    def embed_all(other_ref):
        def one(i, carry):
            embed(other_ref, i)
            return carry

        lax.fori_loop(0, tiles, one, 0)

    def start_own():
        acc_ref[...] = jnp.zeros_like(acc_ref)
        sq_ref[...] = jnp.sum(folded(feat_ref[...]), axis=1, keepdims=True)

    px = [out_ref.at[r, :, :width] for r in range(ROUNDS)]
    plow = [out_ref.at[r, :, width:] for r in range(ROUNDS)]

    pieces = [Piece(p) for p in range(PIECES)]
    length = 7 + last

    def spread(t):
        for p in range(PIECES):
            if 0 <= t - p < length:
                pieces[p].step(t - p)

    load_x.wait()
    load_l.wait()
    gather(0)
    pl.semaphore_wait(barrier, 5)
    steps = length + PIECES - 1
    started = 0
    relayed = 0
    for t in range(steps - 2):
        spread(t)

        if started < CHUNKS and (t % 2 == 1 or t == steps - 3):
            ahead(started).start()
            started += 1
        if t % 2 == 0 and 4 <= t and relayed + 1 < started:
            relay(relayed)
            relayed += 1
        if t == 0:
            gather(1)
        elif t == 1:
            start_own()
        elif t in (2, 3, 4):
            embed(feat_ref, t - 2)

    for c in range(started, CHUNKS):
        ahead(c).start()

    gram0 = dot_nt(px[0][...], px[0][...])
    c0, q0 = diagonals(gram0)
    a_ref[...] = closeness(gram0, c0, q0, width) - dot_nt(plow[0][...], plow[0][...])
    factor_start(m_ref, inv_ref.at[0])
    factor_part(0, a_ref, m_ref, inv_ref.at[0])
    spread(steps - 2)
    relay(relayed)
    factor_part(1, a_ref, m_ref, inv_ref.at[0])
    spread(steps - 1)
    relay(relayed + 1)
    relay(relayed + 2)
    gram1 = dot_nt(px[1][...], px[1][...])
    c1, q1 = diagonals(gram1)
    cross = closeness(dot_nt(px[1][...], px[0][...]), c1, q0, width) - dot_nt(plow[1][...], plow[0][...])
    ext = dot_nt_high(cross, inv_ref[0]).astype(BF16)
    ext_ref[...] = ext
    a_ref[...] = closeness(gram1, c1, q1, width) - dot_nt(plow[1][...], plow[1][...]) - dot_nt(ext, ext)
    factor_start(m_ref, inv_ref.at[1])
    factor_part(0, a_ref, m_ref, inv_ref.at[1])
    relay(relayed + 3)
    relay(relayed + 4)
    factor_part(1, a_ref, m_ref, inv_ref.at[1])
    relay(relayed + 5)

    def extend(i, carry):
        here = pl.ds(pl.multiple_of(i * tile, tile), tile)
        x, tl, sq = feat_ref[here, :], fact_ref[here, :], sq_ref[here, :]
        cross = closeness(dot_nt(x, px[0][...]), sq, q0, width) - dot_nt(tl, plow[0][...])
        new0 = dot_nt_high(cross, inv_ref[0]).astype(BF16)
        cross = closeness(dot_nt(x, px[1][...]), sq, q1, width) - dot_nt(tl, plow[1][...]) - dot_nt(
            new0, ext_ref[...]
        )
        new1 = dot_nt_high(cross, inv_ref[1]).astype(BF16)
        col_ref[here, :piv] = new0
        col_ref[here, piv:] = new1
        sums_ref[:, here] = 1.0 - row_sums(folded(tl) + folded(new0) + folded(new1))
        return carry

    lax.fori_loop(0, tiles, extend, 0)
    for c in range(relayed + 6, CHUNKS):
        relay(c)

    @pl.when(ypos == 0)
    def _():
        for c in range(CHUNKS):
            ahead(c).wait_recv()

    embed_all(second_ref)
    for c in range(CHUNKS):
        across(c, feat_ref).wait_recv()
    embed_all(first_ref)
    means = row_sums(acc_ref[...]) / (3.0 * rows)
    left = sums_ref[...]
    for t in range(rows // 128):
        emb_ref[t:t + 1, :] = means[:, t * 128:(t + 1) * 128]
        left_ref[t:t + 1, :] = left[:, t * 128:(t + 1) * 128]
    for c in range(CHUNKS):
        ahead(c).wait_send()
        across(c, feat_ref).wait_send()


def everything(features, factors, pivots, owners):
    size = lax.axis_size("blk")
    rows, feats = features.shape
    rank = factors.shape[1]
    piv = pivots.shape[1]
    width = feats + rank
    span = width // (PIECES // ROUNDS)
    vmem = pl.BlockSpec(memory_space=pltpu.VMEM)
    anywhere = pl.BlockSpec(memory_space=pl.ANY)
    buffer = lambda count: pltpu.VMEM((PIECES, count, span), BF16)
    copies = lambda *shape: pltpu.SemaphoreType.DMA(shape)
    return pl.pallas_call(
        functools.partial(whole_kernel, size),
        out_shape=(
            jax.ShapeDtypeStruct((rows // 128, 128), F32),
            jax.ShapeDtypeStruct((rows, ROUNDS * piv), BF16),
            jax.ShapeDtypeStruct((rows // 128, 128), F32),
        ),
        in_specs=[anywhere, anywhere, vmem, pl.BlockSpec(memory_space=pltpu.SMEM)],
        out_specs=(vmem, vmem, vmem),
        scratch_shapes=[
            pltpu.VMEM((rows, feats), BF16), pltpu.VMEM((rows, rank), BF16),
            pltpu.VMEM((rows, feats), BF16), pltpu.VMEM((rows, feats), BF16),
            pltpu.VMEM((rows, 128), F32), pltpu.VMEM((rows, 1), F32),
            pltpu.VMEM((ROUNDS, piv, width), BF16), pltpu.VMEM((ROUNDS, piv, width), BF16),
            buffer(piv // 2), buffer(piv // 4), buffer(piv // 8),
            buffer(piv // 2), buffer(piv // 4), buffer(piv // 8),
            buffer(piv // 8), buffer(piv // 8),
            pltpu.VMEM((PIECES, 2, piv // 8, span), BF16),
            pltpu.VMEM((piv, piv), F32), pltpu.VMEM((piv, piv), F32),
            pltpu.VMEM((ROUNDS, piv, piv), F32), pltpu.VMEM((piv, piv), BF16), pltpu.VMEM((1, rows), F32),
            copies(PIECES, 8), copies(PIECES, 8), copies(2),
            copies(CHUNKS), copies(CHUNKS), copies(CHUNKS), copies(CHUNKS),
        ],
        compiler_params=pltpu.CompilerParams(
            vmem_limit_bytes=VMEM_LIMIT, collective_id=0, has_side_effects=True
        ),
        cost_estimate=pl.CostEstimate(flops=12 * 10**9, bytes_accessed=6 * 10**6, transcendentals=0),
        name="everything",
    )(features, factors, pivots, owners)


def on_device(features, factors, pivots, owners):
    rows = features.shape[0]
    embedding, columns, leftover = everything(features, factors, pivots, owners)
    return embedding.reshape(rows), columns, leftover.reshape(rows)


def solution(mesh):
    placed = (P(("blk", "grp"), None), P(("blk", "grp"), None), P(), P())
    return jax.shard_map(
        on_device,
        mesh=mesh,
        in_specs=placed,
        out_specs=(P(("blk", "grp")), P(("blk", "grp"), None), P(("blk", "grp"))),
        check_vma=False,
    )
```

```python
import functools

import jax
import jax.numpy as jnp
from jax import lax
from jax.experimental import pallas as pl
from jax.experimental.pallas import tpu as pltpu
from jax.sharding import PartitionSpec as P

ROUNDS = 2
F32 = jnp.float32
BF16 = jnp.bfloat16
HIGHEST = lax.Precision.HIGHEST
VMEM_LIMIT = 56 * 1024 * 1024
NT = (((1,), (1,)), ((), ()))
TN = (((0,), (0,)), ((), ()))


def dot_nt(a, b):
    return lax.dot_general(a, b, NT, preferred_element_type=F32)


def dot_nt_high(a, b):
    return lax.dot_general(a, b, NT, precision=HIGHEST, preferred_element_type=F32)


def split3(x):
    high = x.astype(BF16).astype(F32)
    rest = x - high
    mid = rest.astype(BF16).astype(F32)
    return high, mid, rest - mid


def factor_start(m_ref, inv_ref):
    n = m_ref.shape[0]
    row = lax.broadcasted_iota(jnp.int32, (n, n), 0)
    col = lax.broadcasted_iota(jnp.int32, (n, n), 1)
    m_ref[...] = (row == col).astype(F32)
    inv_ref[...] = jnp.zeros((n, n), F32)


def factor_part(part, a_ref, m_ref, inv_ref):
    n = a_ref.shape[0]
    half = 128
    sub = lax.broadcasted_iota(jnp.int32, (8, 128), 0)

    left = part * half
    right = left + half
    wide = n - left
    lane = lax.broadcasted_iota(jnp.int32, (8, half), 1)

    def panel(k, carry):
        base = pl.multiple_of(left + k * 8, 8)
        rows = pl.ds(base, 8)
        panel_a = a_ref[rows, left:]
        panel_m = m_ref[rows, :right]
        diag = panel_a[:, :half]
        tiles = [panel_a[:, t * 128:(t + 1) * 128] for t in range(wide // 128)]
        tiles += [panel_m[:, t * 128:(t + 1) * 128] for t in range(right // 128)]
        cols = []
        for j in range(8):
            picked = jnp.where(lane == k * 8 + j, diag, 0.0)
            cols.append(jnp.broadcast_to(jnp.sum(picked, axis=1, keepdims=True), (8, 128)))
        scale = jnp.ones((8, 128), F32)
        for j in range(8):
            pivot = jnp.broadcast_to(cols[j][j:j + 1, :], (8, 128))
            scale = jnp.where(sub == j, pivot, scale)
            if j < 7:
                mult = jnp.where(sub > j, cols[j] / pivot, 0.0)
                for c in range(j + 1, 8):
                    cols[c] = cols[c] - mult * jnp.broadcast_to(cols[c][j:j + 1, :], (8, 128))
                tiles = [t - mult * jnp.broadcast_to(t[j:j + 1, :], (8, 128)) for t in tiles]
        scale = lax.rsqrt(scale)
        tiles = [t * scale for t in tiles]
        q = jnp.concatenate(tiles, axis=1)
        inv_ref[rows, :right] = q[:, wide:]
        h, m, l = split3(q)
        rhs = jnp.concatenate([h, m, h, l, h, m], axis=0).astype(BF16)
        lhs = jnp.concatenate([h, h, m, h, l, m], axis=0)[:, :wide].astype(BF16)
        upd = lax.dot_general(lhs, rhs, TN, preferred_element_type=F32)
        a_ref[left:, left:] = a_ref[left:, left:] - upd[:, :wide]
        m_ref[left:, :right] = m_ref[left:, :right] - upd[:, wide:]
        return carry

    lax.fori_loop(0, half // 8, panel, 0)


def diagonals(gram):
    n = gram.shape[0]
    row = lax.broadcasted_iota(jnp.int32, (n, n), 0)
    col = lax.broadcasted_iota(jnp.int32, (n, n), 1)
    only = jnp.where(row == col, gram, 0.0)
    return jnp.sum(only, axis=1, keepdims=True), jnp.sum(only, axis=0, keepdims=True)


def closeness(gram, left_sq, right_sq, width):
    return jnp.exp((2.0 * gram - left_sq - right_sq) / (8.0 * width))


PIECES = 4
CHUNKS = 12


def folded(x):
    total = None
    for t in range(x.shape[1] // 128):
        wide = x[:, t * 128:(t + 1) * 128].astype(F32)
        total = wide * wide if total is None else total + wide * wide
    return total


def row_sums(lanes):
    return jnp.sum(jnp.transpose(lanes), axis=0, keepdims=True)


def whole_kernel(size, feat_hbm, fact_hbm, piv_ref, own_ref, emb_ref, col_ref, left_ref,
                 feat_ref, fact_ref, second_ref, first_ref, acc_ref, sq_ref, out_ref, g_ref, s1_ref, s2_ref, s3_ref,
                 r0_ref, r1_ref, r2_ref, up_ref, dn_ref, send_ref, a_ref, m_ref, inv_ref, ext_ref, sums_ref,
                 send_sem, recv_sem, load_sem, zsend_sem, zrecv_sem, ysend_sem, yrecv_sem):
    blk, grp = lax.axis_index("blk"), lax.axis_index("grp")
    core, xpos = lax.rem(grp, 2), lax.div(grp, 2)
    ypos, zpos = lax.rem(blk, 2), lax.div(blk, 2)
    last = size // 2 - 1
    mesh = pl.DeviceIdType.MESH
    near_core = (blk, grp + 1 - 2 * core)
    near_x = (blk, grp + 2 - 4 * xpos)
    near_y = (blk + 1 - 2 * ypos, grp)
    above = (lax.rem(blk + 2, size), grp)
    below = (lax.rem(blk + size - 2, size), grp)

    load_x = pltpu.make_async_copy(feat_hbm, feat_ref, load_sem.at[0])
    load_l = pltpu.make_async_copy(fact_hbm, fact_ref, load_sem.at[1])
    load_x.start()
    load_l.start()

    barrier = pltpu.get_barrier_semaphore()
    for other in (near_core, near_x, near_y, above, below):
        pl.semaphore_signal(barrier, inc=1, device_id=other, device_id_type=mesh)

    rows, width = feat_ref.shape
    rank = fact_ref.shape[1]
    piv = piv_ref.shape[1]
    me = blk * lax.axis_size("grp") + grp
    ids = lax.broadcasted_iota(jnp.int32, (rows, piv), 0)

    def gather(rnd):
        mine = jnp.where(own_ref[rnd] == me, 1.0, 0.0)
        pick = jnp.where(ids == piv_ref[rnd:rnd + 1, :], mine, 0.0).astype(BF16)
        g_ref[rnd, :, :width] = lax.dot_general(pick, feat_ref[...], TN, preferred_element_type=F32).astype(BF16)
        g_ref[rnd, :, width:] = lax.dot_general(pick, fact_ref[...], TN, preferred_element_type=F32).astype(BF16)

    per = PIECES // ROUNDS
    span = (width + rank) // per
    half, quarter, eighth = piv // 2, piv // 4, piv // 8

    class Piece:
        def __init__(self, p):
            self.p, self.rnd = p, p // per
            self.cols = pl.ds((p % per) * span, span)
            self.one, self.two = (xpos, near_x), (ypos, near_y)
            self.base1 = core * half
            self.base2 = self.base1 + self.one[0] * quarter
            self.base3 = self.base2 + self.two[0] * eighth

        def copy(self, k, src, dst, device):
            return pltpu.make_async_remote_copy(
                src_ref=src, dst_ref=dst, send_sem=send_sem.at[self.p, k], recv_sem=recv_sem.at[self.p, k],
                device_id=device, device_id_type=mesh)

        def out(self, base, count):
            return out_ref.at[self.rnd, pl.ds(pl.multiple_of(base, 16), count), self.cols]

        def link(self, k):
            p = self.p
            if k == 0:
                src = g_ref.at[self.rnd, pl.ds(pl.multiple_of((1 - core) * half, 16), half), self.cols]
                return self.copy(0, src, r0_ref.at[p], near_core)
            if k == 1:
                src = s1_ref.at[p, pl.ds(pl.multiple_of((1 - self.one[0]) * quarter, 16), quarter)]
                return self.copy(1, src, r1_ref.at[p], self.one[1])
            if k == 2:
                src = s2_ref.at[p, pl.ds(pl.multiple_of((1 - self.two[0]) * eighth, 16), eighth)]
                return self.copy(2, src, r2_ref.at[p], self.two[1])
            if k == 3:
                return self.copy(3, send_ref.at[p, 0], up_ref.at[p], above)
            if k == 4:
                return self.copy(4, send_ref.at[p, 1], dn_ref.at[p], below)
            if k == 5:
                return self.copy(5, self.out(self.base3, eighth), self.out(self.base3, eighth), self.two[1])
            if k == 6:
                return self.copy(6, self.out(self.base2, quarter), self.out(self.base2, quarter), self.one[1])
            return self.copy(7, self.out(self.base1, half), self.out(self.base1, half), near_core)

        def step(self, t):
            p = self.p
            if t == 0:
                self.link(0).start()
            elif t == 1:
                self.link(0).wait_recv()
                rows0 = pl.ds(pl.multiple_of(core * half, 16), half)
                s1_ref[p] = g_ref[self.rnd, rows0, self.cols] + r0_ref[p]
                self.link(1).start()
            elif t == 2:
                self.link(1).wait_recv()
                rows1 = pl.ds(pl.multiple_of(self.one[0] * quarter, 16), quarter)
                s2_ref[p] = s1_ref[p, rows1] + r1_ref[p]
                self.link(2).start()
            elif t == 3:
                self.link(2).wait_recv()
                rows2 = pl.ds(pl.multiple_of(self.two[0] * eighth, 16), eighth)
                s3_ref[p] = s2_ref[p, rows2] + r2_ref[p]

                @pl.when(zpos == 0)
                def _():
                    up_ref[p] = jnp.zeros_like(up_ref[p])
                    send_ref[p, 0] = s3_ref[p]
                    self.link(3).start()

                @pl.when(zpos == last)
                def _():
                    dn_ref[p] = jnp.zeros_like(dn_ref[p])
                    send_ref[p, 1] = s3_ref[p]
                    self.link(4).start()
            elif t < 3 + last:
                hop = t - 3

                @pl.when(zpos == hop)
                def _():
                    self.link(3).wait_recv()
                    send_ref[p, 0] = s3_ref[p] + up_ref[p]
                    self.link(3).start()

                @pl.when(zpos == last - hop)
                def _():
                    self.link(4).wait_recv()
                    send_ref[p, 1] = s3_ref[p] + dn_ref[p]
                    self.link(4).start()
            elif t == 3 + last:
                @pl.when(zpos == last)
                def _():
                    self.link(3).wait_recv()

                @pl.when(zpos == 0)
                def _():
                    self.link(4).wait_recv()

                rows3 = pl.ds(pl.multiple_of(self.base3, 16), eighth)
                out_ref[self.rnd, rows3, self.cols] = s3_ref[p] + up_ref[p] + dn_ref[p]
                self.link(5).start()
            elif t == 4 + last:
                self.link(5).wait_recv()
                self.link(6).start()
            elif t == 5 + last:
                self.link(6).wait_recv()
                self.link(7).start()
            else:
                self.link(7).wait_recv()
                for k in (0, 1, 2, 5, 6, 7):
                    self.link(k).wait_send()

                @pl.when(zpos < last)
                def _():
                    self.link(3).wait_send()

                @pl.when(zpos > 0)
                def _():
                    self.link(4).wait_send()

    chunk = rows // CHUNKS

    def part_of(ref, c):
        return ref.at[pl.ds(c * chunk, chunk)]

    def ahead(c):
        return pltpu.make_async_remote_copy(
            src_ref=part_of(feat_hbm, c), dst_ref=part_of(second_ref, c), send_sem=zsend_sem.at[c],
            recv_sem=zrecv_sem.at[c], device_id=above, device_id_type=mesh)

    def across(c, ref):
        return pltpu.make_async_remote_copy(
            src_ref=part_of(ref, c), dst_ref=part_of(first_ref, c), send_sem=ysend_sem.at[c],
            recv_sem=yrecv_sem.at[c], device_id=near_y, device_id_type=mesh)

    def relay(c):
        if not 0 <= c < CHUNKS:
            return

        @pl.when(ypos == 1)
        def _():
            ahead(c).wait_recv()
            across(c, second_ref).start()

        @pl.when(ypos == 0)
        def _():
            across(c, feat_ref).start()

    tile = 256
    tiles = rows // tile

    def embed(other_ref, i):
        part = other_ref[pl.ds(i * tile, tile), :]
        e = closeness(dot_nt(feat_ref[...], part), sq_ref[...], row_sums(folded(part)), width)
        for t in range(tile // 128):
            acc_ref[...] += e[:, t * 128:(t + 1) * 128]

    def embed_all(other_ref):
        def one(i, carry):
            embed(other_ref, i)
            return carry

        lax.fori_loop(0, tiles, one, 0)

    def start_own():
        acc_ref[...] = jnp.zeros_like(acc_ref)
        sq_ref[...] = jnp.sum(folded(feat_ref[...]), axis=1, keepdims=True)

    px = [out_ref.at[r, :, :width] for r in range(ROUNDS)]
    plow = [out_ref.at[r, :, width:] for r in range(ROUNDS)]

    pieces = [Piece(p) for p in range(PIECES)]
    length = 7 + last

    def spread(t):
        for p in range(PIECES):
            if 0 <= t - p < length:
                pieces[p].step(t - p)

    load_x.wait()
    load_l.wait()
    gather(0)
    pl.semaphore_wait(barrier, 5)
    steps = length + PIECES - 1
    started = 0
    relayed = 0
    for t in range(steps - 2):
        spread(t)

        if started < CHUNKS and (t % 2 == 1 or t == steps - 3):
            ahead(started).start()
            started += 1
        if t % 2 == 0 and 4 <= t and relayed + 1 < started:
            relay(relayed)
            relayed += 1
        if t == 0:
            gather(1)
        elif t == 1:
            start_own()
        elif t in (2, 3, 4):
            embed(feat_ref, t - 2)

    for c in range(started, CHUNKS):
        ahead(c).start()

    gram0 = dot_nt(px[0][...], px[0][...])
    c0, q0 = diagonals(gram0)
    a_ref[...] = closeness(gram0, c0, q0, width) - dot_nt(plow[0][...], plow[0][...])
    factor_start(m_ref, inv_ref.at[0])
    factor_part(0, a_ref, m_ref, inv_ref.at[0])
    spread(steps - 2)
    relay(relayed)
    factor_part(1, a_ref, m_ref, inv_ref.at[0])
    spread(steps - 1)
    relay(relayed + 1)
    relay(relayed + 2)
    gram1 = dot_nt(px[1][...], px[1][...])
    c1, q1 = diagonals(gram1)
    cross = closeness(dot_nt(px[1][...], px[0][...]), c1, q0, width) - dot_nt(plow[1][...], plow[0][...])
    ext = dot_nt_high(cross, inv_ref[0]).astype(BF16)
    ext_ref[...] = ext
    a_ref[...] = closeness(gram1, c1, q1, width) - dot_nt(plow[1][...], plow[1][...]) - dot_nt(ext, ext)
    factor_start(m_ref, inv_ref.at[1])
    factor_part(0, a_ref, m_ref, inv_ref.at[1])
    relay(relayed + 3)
    relay(relayed + 4)
    factor_part(1, a_ref, m_ref, inv_ref.at[1])
    relay(relayed + 5)

    def extend(i, carry):
        here = pl.ds(pl.multiple_of(i * tile, tile), tile)
        x, tl, sq = feat_ref[here, :], fact_ref[here, :], sq_ref[here, :]
        cross = closeness(dot_nt(x, px[0][...]), sq, q0, width) - dot_nt(tl, plow[0][...])
        new0 = dot_nt_high(cross, inv_ref[0]).astype(BF16)
        cross = closeness(dot_nt(x, px[1][...]), sq, q1, width) - dot_nt(tl, plow[1][...]) - dot_nt(
            new0, ext_ref[...]
        )
        new1 = dot_nt_high(cross, inv_ref[1]).astype(BF16)
        col_ref[here, :piv] = new0
        col_ref[here, piv:] = new1
        sums_ref[:, here] = 1.0 - row_sums(folded(tl) + folded(new0) + folded(new1))
        return carry

    lax.fori_loop(0, 1, extend, 0)
    relay(relayed + 6)
    lax.fori_loop(1, tiles, extend, 0)
    for c in range(relayed + 7, CHUNKS):
        relay(c)

    @pl.when(ypos == 0)
    def _():
        for c in range(CHUNKS):
            ahead(c).wait_recv()

    embed_all(second_ref)
    for i in range(tiles):
        for c in range(i * CHUNKS // tiles, (i + 1) * CHUNKS // tiles):
            across(c, feat_ref).wait_recv()
        embed(first_ref, i)
    means = row_sums(acc_ref[...]) / (3.0 * rows)
    left = sums_ref[...]
    for t in range(rows // 128):
        emb_ref[t:t + 1, :] = means[:, t * 128:(t + 1) * 128]
        left_ref[t:t + 1, :] = left[:, t * 128:(t + 1) * 128]
    for c in range(CHUNKS):
        ahead(c).wait_send()
        across(c, feat_ref).wait_send()


def everything(features, factors, pivots, owners):
    size = lax.axis_size("blk")
    rows, feats = features.shape
    rank = factors.shape[1]
    piv = pivots.shape[1]
    width = feats + rank
    span = width // (PIECES // ROUNDS)
    vmem = pl.BlockSpec(memory_space=pltpu.VMEM)
    anywhere = pl.BlockSpec(memory_space=pl.ANY)
    buffer = lambda count: pltpu.VMEM((PIECES, count, span), BF16)
    copies = lambda *shape: pltpu.SemaphoreType.DMA(shape)
    return pl.pallas_call(
        functools.partial(whole_kernel, size),
        out_shape=(
            jax.ShapeDtypeStruct((rows // 128, 128), F32),
            jax.ShapeDtypeStruct((rows, ROUNDS * piv), BF16),
            jax.ShapeDtypeStruct((rows // 128, 128), F32),
        ),
        in_specs=[anywhere, anywhere, vmem, pl.BlockSpec(memory_space=pltpu.SMEM)],
        out_specs=(vmem, vmem, vmem),
        scratch_shapes=[
            pltpu.VMEM((rows, feats), BF16), pltpu.VMEM((rows, rank), BF16),
            pltpu.VMEM((rows, feats), BF16), pltpu.VMEM((rows, feats), BF16),
            pltpu.VMEM((rows, 128), F32), pltpu.VMEM((rows, 1), F32),
            pltpu.VMEM((ROUNDS, piv, width), BF16), pltpu.VMEM((ROUNDS, piv, width), BF16),
            buffer(piv // 2), buffer(piv // 4), buffer(piv // 8),
            buffer(piv // 2), buffer(piv // 4), buffer(piv // 8),
            buffer(piv // 8), buffer(piv // 8),
            pltpu.VMEM((PIECES, 2, piv // 8, span), BF16),
            pltpu.VMEM((piv, piv), F32), pltpu.VMEM((piv, piv), F32),
            pltpu.VMEM((ROUNDS, piv, piv), F32), pltpu.VMEM((piv, piv), BF16), pltpu.VMEM((1, rows), F32),
            copies(PIECES, 8), copies(PIECES, 8), copies(2),
            copies(CHUNKS), copies(CHUNKS), copies(CHUNKS), copies(CHUNKS),
        ],
        compiler_params=pltpu.CompilerParams(
            vmem_limit_bytes=VMEM_LIMIT, collective_id=0, has_side_effects=True
        ),
        cost_estimate=pl.CostEstimate(flops=12 * 10**9, bytes_accessed=6 * 10**6, transcendentals=0),
        name="everything",
    )(features, factors, pivots, owners)


def on_device(features, factors, pivots, owners):
    rows = features.shape[0]
    embedding, columns, leftover = everything(features, factors, pivots, owners)
    return embedding.reshape(rows), columns, leftover.reshape(rows)


def solution(mesh):
    placed = (P(("blk", "grp"), None), P(("blk", "grp"), None), P(), P())
    return jax.shard_map(
        on_device,
        mesh=mesh,
        in_specs=placed,
        out_specs=(P(("blk", "grp")), P(("blk", "grp"), None), P(("blk", "grp"))),
        check_vma=False,
    )
```
